32 devices in a mesh: band: 8 (over z, y), mp: 4 (over x, core).
Axes of the slice: x: 2, y: 2, z: 4, core: 2. Of those that a mesh axis runs over, the one named last changes fastest.
Arguments:
- cells: bfloat16 [2048, 1024], P('band', 'mp'), may hold values from -81 to 81
- row_gain: float32 [1024], replicated, may hold values from 0.1 to 1.9
- row_qkv: bfloat16 [3, 1024, 1024], P(None, None, 'mp'), may hold values from -1.25 to 1.25
- row_out: bfloat16 [1024, 1024], P('mp'), may hold values from -0.1875 to 0.1875
- col_gain: float32 [1024], replicated, may hold values from 0.1 to 1.9
- col_qkv: bfloat16 [3, 1024, 1024], P(None, None, 'mp'), may hold values from -1.25 to 1.25
- col_out: bfloat16 [1024, 1024], P('mp'), may hold values from -0.1875 to 0.1875
- row_seg: int32 [2048], P('band'), may hold values from 0 to 255, never falling along the last dimension, each value on 1 to 16 neighbouring positions
- col_dest: int32 [2048, 1], P('band'), may hold values from 0 to 7; in each aligned block of 256 rows (0 to 255, 256 to 511, ...) at most 48 rows name the same one
- sheet_column_index: int32 [2048], P('band'), may hold values from 1 to 8
- d_result: bfloat16 [2048, 1024], P('band', 'mp'), may hold values from -6 to 6
Outputs:
- result: bfloat16 [2048, 1024], P('band', 'mp')
- d_cells: bfloat16 [2048, 1024], P('band', 'mp')
The draws below stay inside these ranges and needn't reach their ends.
Inputs may be any that keep to these rules, and one draw needn't show every extreme that they name: `row_seg`: cells never fall in value along the array. `col_dest`: at most 48 of the cells of one row band name the same column band, and some row band sends exactly 48 to some column band.
All inputs are finite; a program needn't handle non-finite values.
Results may differ from the reference program's by a relative error of at most 0.019.
Values may be sent and summed in bfloat16 or wider, within the bound.
A program may use at most 64 MiB of HBM per device.

```python
import math
from functools import partial
import jax
import jax.numpy as jnp
import numpy as np
from jax import lax

D = 1024
HEAD_DIM = 64
CELLS_DEV = 256
TILE = 128
COLS = 8
CAP = 48
COL_SLOTS = 384
CELLS = 2048
ROW_SEGS = 256
N_BAND = 8
N_MP = 4


def draw_cells(key, part):
    inner = jax.random.fold_in(key, 13)
    first, second, third = jax.random.split(inner, 3)
    base = jnp.clip(jax.random.normal(first, (CELLS, D), jnp.float32), -4.0, 4.0)
    row_scale = jnp.exp(jax.random.uniform(second, (CELLS, 1), jnp.float32, 0.0, math.log(10.0)))
    col_scale = jnp.exp(jax.random.uniform(third, (1, D), jnp.float32, -0.69, 0.69))
    return (base * row_scale * col_scale).astype(jnp.bfloat16)


def draw_row_qkv(key, part):
    inner = jax.random.fold_in(key, 11)
    base = jnp.clip(jax.random.normal(inner, (3, D, D), jnp.float32), -4.0, 4.0) * D ** (-0.5)
    return base.astype(jnp.bfloat16)


def draw_col_qkv(key, part):
    inner = jax.random.fold_in(key, 12)
    base = jnp.clip(jax.random.normal(inner, (3, D, D), jnp.float32), -4.0, 4.0) * D ** (-0.5)
    return base.astype(jnp.bfloat16)


def set_ends(values, key, smallest, largest):
    index_at = [jax.random.randint(jax.random.fold_in(key, axis), (), 0, length) for axis, length in enumerate(values.shape)]
    widest = values.shape.index(max(values.shape))
    neighbour = index_at[:widest] + [(index_at[widest] + 1) % values.shape[widest]] + index_at[widest + 1:]
    return values.at[tuple(index_at)].set(smallest).at[tuple(neighbour)].set(largest)


def shard_levels(key, shape, shards, low, high):
    loudness, own = 1.0, jax.random.fold_in(key, 6)
    for dim, shards_of in shards:
        heights = jnp.exp(jax.random.uniform(jax.random.fold_in(own, dim), (shards_of,), jnp.float32, low / len(shards), high / len(shards)))
        loudness = loudness * jnp.repeat(heights, shape[dim] // shards_of).reshape([-1 if axis == dim else 1 for axis in range(len(shape))])
    return loudness


def length_profile(amount, total, reach, lean):
    weights = [(1 << 20) // math.isqrt(grade ** lean) + 1 for grade in range(2, amount + 1)]
    spare, counts = total - reach - (amount - 1), [1] * (amount - 1)
    while spare > 0:
        movable = [i for i in range(amount - 1) if counts[i] < reach]
        mass, remaining = sum([weights[i] for i in movable]), spare
        for i in movable:
            extra = min(reach - counts[i], max(1, remaining * weights[i] // mass), spare)
            counts[i] = counts[i] + extra
            spare = spare - extra
    return np.array([reach] + counts)


def ragged_sizes(rng, number_of, total, most, skew):
    if number_of == 2:
        one = jax.random.randint(rng, (), max(1, total - most), min(most, total - 1) + 1)
        return jnp.stack([one, total - one])
    tallies = jnp.asarray(length_profile(number_of, total, most, skew), jnp.int32)
    pairs = (number_of - 1) // 2
    giver, taker = tallies[1:1 + 2 * pairs:2], tallies[2:2 + 2 * pairs:2]
    margin = jnp.minimum(giver - 1, most - taker)
    passed = jax.random.randint(jax.random.fold_in(rng, 1), (pairs,), 0, 1 << 20) % (margin + 1)
    tallies = tallies.at[1:1 + 2 * pairs:2].set(giver - passed).at[2:2 + 2 * pairs:2].set(taker + passed)
    return tallies[jax.random.permutation(jax.random.fold_in(rng, 2), number_of)]


def assign_block(stream_key, own, number, rows, count, top, limit, lean):
    sequence = jax.random.permutation(stream_key, count)
    heavy_load, common = shares(count, rows * top, limit, lean, True), shares(count, rows * top, limit, lean, False)
    places = jnp.arange(count)

    def named(tallies, rotation):
        used = int((tallies > 0).sum())
        fixed = max(1, used // 4)
        moved = fixed + (places - fixed + rotation * (used - fixed)) % max(1, count - fixed)
        return jnp.zeros((count,), jnp.int32).at[sequence[jnp.where(places < fixed, places, moved)]].set(jnp.asarray(tallies, jnp.int32))

    tallies = jnp.where(number % 4 == 0, named(heavy_load, number // 4), named(common, number - number // 4 - 1))
    mixed = jax.random.permutation(jax.random.fold_in(own, 3), count)
    source_of, receiver = mixed[0:count // 2 * 2:2], mixed[1:count // 2 * 2:2]
    room = jnp.minimum(tallies[source_of] - 1, limit - tallies[receiver]) // 2
    room = jnp.where((source_of == sequence[0]) | (receiver == sequence[0]) | (tallies[receiver] == 0), 0, jnp.maximum(room, 0))
    moved = jax.random.randint(jax.random.fold_in(own, 4), (count // 2,), 0, 1 << 20) % (room + 1)
    tallies = tallies.at[source_of].add(-moved).at[receiver].add(moved)
    members = jnp.searchsorted(jnp.cumsum(tallies), jnp.arange(rows * top), side="right").astype(jnp.int32)
    listing = members.reshape(top, rows).T
    listing = listing[jax.random.permutation(jax.random.fold_in(own, 1), rows)]
    rotation = jax.random.randint(jax.random.fold_in(own, 2), (rows, 1), 0, top)
    return jnp.take_along_axis(listing, (jnp.arange(top)[None, :] + rotation) % top, axis=1)


def shares(number_of, total, limit, slope, full):
    loads = [(1 << 20) // math.isqrt(rank ** slope) + 1 for rank in range(1, number_of + 1)]
    largest = limit if full else min(limit, max(-(-total // number_of), total * loads[0] // sum(loads)))
    least = 1 if total - largest >= number_of - 1 else 0
    given, surplus = [largest] + [least] * (number_of - 1), total - largest - least * (number_of - 1)
    while surplus > 0:
        free = [i for i in range(1, number_of) if given[i] < largest] or [i for i in range(1, number_of) if given[i] < limit]
        whole, left = sum([loads[i] for i in free]), surplus
        for i in free:
            extra = min(limit - given[i], max(1, left * loads[i] // whole), surplus)
            given[i] = given[i] + extra
            surplus = surplus - extra
    return np.array(given)


def scatter_about(key, extent, width, bound, cuts=(), held_as=jnp.bfloat16):
    entries = jax.random.normal(key, extent, jnp.float32) * width
    if len(cuts) > 0:
        entries = shard_levels(key, extent, cuts, -0.22, 0.18) * entries
    return jnp.clip(entries, min=-bound, max=bound).astype(held_as)


def setup_inputs(seed: int = 0) -> dict:
    streams_of = jax.random.split(jax.random.key(seed), 12)
    cells = draw_cells(jax.random.fold_in(streams_of[11], 71), 0)
    row_gain = jnp.clip(1.0 + 0.18 * jax.random.normal(streams_of[1], (D,), jnp.float32), 0.1, 1.9)
    row_qkv = draw_row_qkv(jax.random.fold_in(streams_of[11], 71), 0)
    row_out = scatter_about(streams_of[3], (D, D), D ** -0.5, 0.1875, ((0, 4),))
    col_gain = jnp.clip(1.0 + 0.18 * jax.random.normal(streams_of[4], (D,), jnp.float32), 0.1, 1.9)
    col_qkv = draw_col_qkv(jax.random.fold_in(streams_of[11], 71), 0)
    col_out = scatter_about(streams_of[6], (D, D), D ** -0.5, 0.1875, ((0, 4),))
    row_seg = jnp.searchsorted(jnp.cumsum(ragged_sizes(streams_of[7], ROW_SEGS, CELLS, 16, 2)), jnp.arange(CELLS), side="right").astype(jnp.int32)
    col_dest_keys = jax.random.split(jax.random.fold_in(streams_of[8], 1), CELLS // CELLS_DEV)
    col_dest_turns = jax.random.permutation(jax.random.fold_in(streams_of[8], 3), CELLS // CELLS_DEV)
    col_dest = jax.vmap(lambda own, number: assign_block(jax.random.fold_in(streams_of[8], 2), own, number, CELLS_DEV, N_BAND, 1, CAP, 2))(col_dest_keys, col_dest_turns).reshape((CELLS, 1))
    sheet_column_index = set_ends(jax.random.randint(streams_of[9], (CELLS,), 1, COLS + 1), jax.random.fold_in(streams_of[9], 1), 1, COLS).astype(jnp.int32)
    d_result = scatter_about(streams_of[10], (CELLS, D), 1.0, 6.0, ((0, 8), (1, 4)))
    return {"cells": cells, "row_gain": row_gain, "row_qkv": row_qkv, "row_out": row_out, "col_gain": col_gain, "col_qkv": col_qkv, "col_out": col_out, "row_seg": row_seg, "col_dest": col_dest, "sheet_column_index": sheet_column_index, "d_result": d_result}


norm_eps = 1e-06
neg_fill = -1e+30

def block_terms(inputs, norm_gain, query_key_value_weight, w_out, allowed, tile_rows):
    values = inputs.astype(jnp.float32)
    inv_rms = lax.rsqrt(lax.optimization_barrier(jnp.mean(values * values, axis=-1, keepdims=True)) + norm_eps)
    normalized_cells = (values * inv_rms * norm_gain).astype(jnp.bfloat16)
    projected_heads = jnp.einsum('lu,xuh->xlh', normalized_cells, query_key_value_weight, preferred_element_type=jnp.float32).astype(jnp.bfloat16)
    row_count = inputs.shape[0]
    feat_width = query_key_value_weight.shape[2]
    head_count = feat_width // HEAD_DIM
    shaped = projected_heads.reshape(3, row_count // tile_rows, tile_rows, head_count, HEAD_DIM)
    scores = jnp.einsum('bqhe,bkhe->bhqk', shaped[0], shaped[1], preferred_element_type=jnp.float32) * HEAD_DIM ** (-0.5)
    scores = jnp.where(allowed[:, None], scores, neg_fill)
    scores = scores - lax.stop_gradient(lax.optimization_barrier(jnp.max(scores, axis=-1, keepdims=True)))
    expd = jnp.exp(scores)
    attn_probs = (expd / lax.optimization_barrier(jnp.sum(expd, axis=-1, keepdims=True))).astype(jnp.bfloat16)
    attended = jnp.einsum('bhqk,bkhe->bqhe', attn_probs, shaped[2], preferred_element_type=jnp.float32).astype(jnp.bfloat16)
    attended = attended.reshape(row_count, feat_width)
    return jnp.dot(attended, w_out, preferred_element_type=jnp.float32)

def group_weights(query_key_value_weight, w_out, group):
    group_width = D // N_MP
    return (query_key_value_weight[:, :, group * group_width:(group + 1) * group_width], w_out[group * group_width:(group + 1) * group_width])

def forward_block(inputs, norm_gain, query_key_value_weight, w_out, allowed, tile_rows):
    accum_sum = jnp.zeros(inputs.shape, jnp.float32)
    for group in range(N_MP):
        part_qkv, part_out = group_weights(query_key_value_weight, w_out, group)
        term = block_terms(inputs, norm_gain, part_qkv, part_out, allowed, tile_rows).astype(jnp.bfloat16)
        accum_sum = accum_sum + lax.optimization_barrier(term).astype(jnp.float32)
    return (inputs.astype(jnp.float32) + accum_sum).astype(jnp.bfloat16)

def backward_block(inputs, d_out, norm_gain, query_key_value_weight, w_out, allowed, tile_rows):
    accum_sum = jnp.zeros(inputs.shape, jnp.float32)
    for group in range(N_MP):
        part_qkv, part_out = group_weights(query_key_value_weight, w_out, group)
        local_fn = partial(block_terms, norm_gain=norm_gain, query_key_value_weight=part_qkv, w_out=part_out, allowed=allowed, tile_rows=tile_rows)
        _, pull_back = jax.vjp(local_fn, inputs)
        d_part, = pull_back(d_out.astype(jnp.float32))
        accum_sum = accum_sum + d_part.astype(jnp.float32)
    return (d_out.astype(jnp.float32) + accum_sum).astype(jnp.bfloat16)

def column_band_mask(col_keys):
    positions = jnp.arange(col_keys.shape[0])
    same_col = (col_keys[:, None] == col_keys[None, :]) & (col_keys[None, :] > 0)
    return (same_col | (positions[:, None] == positions[None, :]))[None]

def reference(cells, row_gain, row_qkv, row_out, col_gain, col_qkv, col_out, row_seg, col_dest, sheet_column_index, d_result):
    row_groups = row_seg.reshape(CELLS // TILE, TILE)
    row_mask = row_groups[:, :, None] == row_groups[:, None, :]
    mixed_rows = forward_block(cells, row_gain, row_qkv, row_out, row_mask, TILE)
    target = col_dest[:, 0].reshape(N_BAND, CELLS_DEV)
    onehot = (target[:, :, None] == jnp.arange(N_BAND, dtype=jnp.int32)[None, None, :]).astype(jnp.int32)
    ranking = lax.optimization_barrier(jnp.sum((jnp.cumsum(onehot, axis=1) - onehot) * onehot, axis=-1))
    sources = jnp.arange(N_BAND, dtype=jnp.int32)[:, None]
    position = (target * COL_SLOTS + sources * CAP + ranking).reshape(-1).astype(jnp.int32)
    colbuf = jnp.zeros((N_BAND * COL_SLOTS, D), jnp.bfloat16).at[position].set(mixed_rows).reshape(N_BAND, COL_SLOTS, D)
    colkey = jnp.zeros((N_BAND * COL_SLOTS,), jnp.int32).at[position].set(sheet_column_index.astype(jnp.int32)).reshape(N_BAND, COL_SLOTS)

    def column_attention_forward(pieces):
        inputs, col_keys = pieces
        return forward_block(inputs, col_gain, col_qkv, col_out, column_band_mask(col_keys), COL_SLOTS)
    settled = lax.map(column_attention_forward, (colbuf, colkey))
    result = settled.reshape(N_BAND * COL_SLOTS, D)[position]
    d_colbuf = jnp.zeros((N_BAND * COL_SLOTS, D), jnp.bfloat16).at[position].set(d_result).reshape(N_BAND, COL_SLOTS, D)

    def column_attention_backward(pieces):
        inputs, d_out, col_keys = pieces
        return backward_block(inputs, d_out, col_gain, col_qkv, col_out, column_band_mask(col_keys), COL_SLOTS)
    d_mixed_col = lax.map(column_attention_backward, (colbuf, d_colbuf, colkey))
    d_mixed = d_mixed_col.reshape(N_BAND * COL_SLOTS, D)[position]
    d_cells = backward_block(cells, d_mixed, row_gain, row_qkv, row_out, row_mask, TILE)
    return (result, d_cells)
```

```python
import jax
import jax.numpy as jnp
from jax import lax
from jax.sharding import PartitionSpec as P

HEAD_DIM = 64
TILE = 128


norm_eps = 1e-06
neg_fill = -1e30


def block_terms(inputs, norm_gain, query_key_value_weight, w_out, allowed, tile_rows):
    values = inputs.astype(jnp.float32)
    inv_rms = lax.rsqrt(jnp.mean(values * values, axis=-1, keepdims=True) + norm_eps)
    normalized_cells = (values * inv_rms * norm_gain).astype(jnp.bfloat16)
    projected_heads = jnp.einsum(
        "lu,xuh->xlh", normalized_cells, query_key_value_weight, preferred_element_type=jnp.float32
    ).astype(jnp.bfloat16)
    row_count = inputs.shape[0]
    feat_width = query_key_value_weight.shape[2]
    head_count = feat_width // HEAD_DIM
    shaped = projected_heads.reshape(3, row_count // tile_rows, tile_rows, head_count, HEAD_DIM)
    scores = jnp.einsum(
        "bqhe,bkhe->bhqk", shaped[0], shaped[1], preferred_element_type=jnp.float32
    ) * HEAD_DIM ** (-0.5)
    scores = jnp.where(allowed[:, None], scores, neg_fill)
    scores = scores - lax.stop_gradient(jnp.max(scores, axis=-1, keepdims=True))
    expd = jnp.exp(scores)
    attn_probs = (expd / jnp.sum(expd, axis=-1, keepdims=True)).astype(jnp.bfloat16)
    attended = jnp.einsum(
        "bhqk,bkhe->bqhe", attn_probs, shaped[2], preferred_element_type=jnp.float32
    ).astype(jnp.bfloat16)
    attended = attended.reshape(row_count, feat_width)
    return jnp.dot(attended, w_out, preferred_element_type=jnp.float32)


def column_band_mask(col_keys):
    positions = jnp.arange(col_keys.shape[0])
    same_col = (col_keys[:, None] == col_keys[None, :]) & (col_keys[None, :] > 0)
    return (same_col | (positions[:, None] == positions[None, :]))[None]


def widen(block):
    return lax.all_gather(block, "mp", axis=1, tiled=True)


def narrow(terms):
    return lax.psum_scatter(
        terms.astype(jnp.bfloat16), "mp", scatter_dimension=1, tiled=True
    ).astype(jnp.float32)


def move_rows(rows):
    return lax.all_to_all(rows, "band", split_axis=0, concat_axis=0, tiled=True)


def on_device(
    cells,
    row_gain,
    row_qkv,
    row_out,
    col_gain,
    col_qkv,
    col_out,
    row_seg,
    col_dest,
    sheet_column_index,
    d_result,
):
    cell_rows, feat_width = cells.shape
    band_count = lax.axis_size("band")
    capacity = max(2, 3 * cell_rows // (2 * band_count))
    slot_total = band_count * capacity
    gathered = widen(cells)
    row_groups = row_seg.reshape(cell_rows // TILE, TILE)
    row_mask = row_groups[:, :, None] == row_groups[:, None, :]

    def row_local(inputs):
        return block_terms(inputs, row_gain, row_qkv, row_out, row_mask, TILE)

    row_terms, row_pull = jax.vjp(row_local, gathered)
    target = col_dest[:, 0]
    place = jnp.arange(cell_rows, dtype=jnp.int32)
    earlier = (target[:, None] == target[None, :]) & (place[None, :] < place[:, None])
    ranking = jnp.sum(earlier.astype(jnp.int32), axis=1)
    slot_index = target * capacity + ranking
    keys_out = (
        jnp.zeros((slot_total,), jnp.bfloat16)
        .at[slot_index]
        .set(sheet_column_index.astype(jnp.bfloat16))
    )
    back_in = jnp.zeros((slot_total, feat_width), jnp.bfloat16).at[slot_index].set(d_result)
    mixed_rows = (cells.astype(jnp.float32) + narrow(row_terms)).astype(jnp.bfloat16)
    outgoing = jnp.zeros((slot_total, feat_width), jnp.bfloat16).at[slot_index].set(mixed_rows)
    arrived, col_keys = (
        lax.all_to_all(outgoing, "band", split_axis=0, concat_axis=0, tiled=True),
        lax.all_to_all(keys_out, "band", split_axis=0, concat_axis=0, tiled=True),
    )
    column_full = widen(arrived)
    col_allowed = column_band_mask(col_keys)

    def col_local(inputs):
        return block_terms(inputs, col_gain, col_qkv, col_out, col_allowed, inputs.shape[0])

    col_terms, col_pull = jax.vjp(col_local, column_full)
    settled = (arrived.astype(jnp.float32) + narrow(col_terms)).astype(jnp.bfloat16)
    result = move_rows(settled)[slot_index]
    d_column = move_rows(back_in)
    (d_col_part,) = col_pull(widen(d_column).astype(jnp.float32))
    d_mixed_col = (d_column.astype(jnp.float32) + narrow(d_col_part.astype(jnp.float32))).astype(
        jnp.bfloat16
    )
    d_mixed = move_rows(d_mixed_col)[slot_index]
    (d_row_part,) = row_pull(widen(d_mixed).astype(jnp.float32))
    d_cells = (d_mixed.astype(jnp.float32) + narrow(d_row_part.astype(jnp.float32))).astype(
        jnp.bfloat16
    )
    return (result, d_cells)


def solution(mesh):
    in_specs = (
        P("band", "mp"),
        P(),
        P(None, None, "mp"),
        P("mp", None),
        P(),
        P(None, None, "mp"),
        P("mp", None),
        P("band"),
        P("band", None),
        P("band"),
        P("band", "mp"),
    )
    out_specs = (P("band", "mp"), P("band", "mp"))
    return jax.shard_map(
        on_device, mesh=mesh, in_specs=in_specs, out_specs=out_specs, check_vma=False
    )
```

```python
import functools

import jax
import jax.numpy as jnp
from jax import lax
from jax.experimental import pallas as pl
from jax.experimental.pallas import tpu as pltpu
from jax.sharding import PartitionSpec as P

HEAD_DIM = 64
TILE = 128


norm_eps = 1e-06
neg_fill = -1e30

MESH = pl.DeviceIdType.MESH
KEY_LANES = 128
f32, bf16 = jnp.float32, jnp.bfloat16


def dot(a, b):
    return lax.dot_general(a, b, (((1,), (0,)), ((), ())), preferred_element_type=f32)


def dot_nt(a, b):
    return lax.dot_general(a, b, (((1,), (1,)), ((), ())), preferred_element_type=f32)


def dot_tn(a, b):
    return lax.dot_general(a, b, (((0,), (0,)), ((), ())), preferred_element_type=f32)


def fused_kernel(
    bands, cap,
    cells, d_result, row_gain, col_gain, seg, dest, key, rw_any, ro_any, cw_any, co_any,
    result, d_cells,
    rw, ro, cw, co, xr, xc, dxc, dxr, e_out, e_in,
    d_out_buf, m_out, s_out, g_out, s_back, g_back,
    r_sib, r_got, r_x, r_xgot, c_sib, c_got, c_x, c_xgot,
    b_sib, b_got, b_x, b_xgot, q_sib, q_got, q_x, q_xgot,
    p_row, p_col, dn_row, dn_col,
    w_sem, ag_send, ag_recv, rs_send, rs_recv, aa_send, aa_recv,
):
    rows, width = cells.shape
    groups = xr.shape[0]
    slots = bands * cap
    heads = width // HEAD_DIM
    features = groups * width
    band, me = lax.axis_index("band"), lax.axis_index("mp")
    near = me + 1 - 2 * lax.rem(me, 2)
    far = lax.rem(me + 2, 4)
    corner = lax.rem(near + 2, 4)
    pending = []

    loads = []
    for i, (src, dst) in enumerate(((rw_any, rw), (ro_any, ro), (cw_any, cw), (co_any, co))):
        load = pltpu.make_async_copy(src, dst, w_sem.at[i])
        load.start()
        loads.append(load)

    xr[me] = cells[...]

    barrier = pltpu.get_barrier_semaphore()
    for peer in (near, far):
        pl.semaphore_signal(barrier, inc=1, device_id=(band, peer), device_id_type=MESH)
    for d in range(1, bands):
        pl.semaphore_signal(
            barrier, inc=1, device_id=(lax.rem(band + d, bands), me), device_id_type=MESH
        )
    pl.semaphore_wait(barrier, bands + 1)

    def send(src, dst, send_sem, recv_sem, to):
        copy = pltpu.make_async_remote_copy(
            src_ref=src, dst_ref=dst, send_sem=send_sem, recv_sem=recv_sem,
            device_id=to, device_id_type=MESH,
        )
        copy.start()
        pending.append(copy)
        return copy

    def spread_start(buf, n):
        across = send(buf.at[me], buf.at[me], ag_send.at[n, 0], ag_recv.at[n, 0], (band, far))
        beside = send(buf.at[me], buf.at[me], ag_send.at[n, 1], ag_recv.at[n, 1], (band, near))
        return across, beside

    def spread_relay(buf, n, started):
        across, beside = started
        across.wait_recv()
        relay = send(buf.at[far], buf.at[far], ag_send.at[n, 2], ag_recv.at[n, 2], (band, near))
        return beside, relay

    def spread_wait(copies):
        for copy in copies:
            copy.wait_recv()

    def exchange_start(src, dst_at, n):
        copies = []
        for d in range(1, bands):
            to = lax.rem(band + d, bands)
            copies.append(
                send(src.at[pl.ds(pl.multiple_of(to * cap, 16), cap)], dst_at(band),
                     aa_send.at[n, d], aa_recv.at[n, d], (to, me))
            )
        dst_at(band)[...] = src[pl.ds(pl.multiple_of(band * cap, 16), cap), :]
        return copies

    def exchange_wait(copies):
        for copy in copies:
            copy.wait_recv()

    def chunk(ref):
        return lambda s: ref.at[pl.ds(pl.multiple_of(s * cap, 16), cap)]

    def inner_chunk(ref):
        return lambda s: ref.at[me, pl.ds(pl.multiple_of(s * cap, 16), cap)]

    def sum_start(part, bufs, n):
        sib, got, _, _ = bufs
        sib[0] = part(corner).astype(bf16)
        a = send(sib.at[0], got.at[0], rs_send.at[n, 0], rs_recv.at[n, 0], (band, near))
        sib[1] = part(near).astype(bf16)
        b = send(sib.at[1], got.at[1], rs_send.at[n, 1], rs_recv.at[n, 1], (band, near))
        return a, b, part(far)

    def sum_cross(bufs, n, state):
        _, got, out, arrived = bufs
        a, b, mine = state
        a.wait_recv()
        out[...] = (mine + got[0].astype(f32)).astype(bf16)
        c = send(out, arrived, rs_send.at[n, 2], rs_recv.at[n, 2], (band, far))
        return b, c

    def sum_end(part, bufs, state):
        _, got, _, arrived = bufs
        b, c = state
        own = part(me).astype(bf16).astype(f32)
        b.wait_recv()
        own = own + got[1].astype(f32)
        c.wait_recv()
        return own + arrived[...].astype(f32)

    def lanes(c):
        return pl.ds(pl.multiple_of(c * width, 128), width)

    def project(x, gain, w):
        total = jnp.zeros((x.shape[1], 1), f32)
        for c in range(groups):
            v = x[c].astype(f32)
            total = total + jnp.sum(v * v, axis=-1, keepdims=True)
        inv = lax.rsqrt(total / features + norm_eps)
        acc = [None] * 3
        for c in range(groups):
            n = (x[c].astype(f32) * inv * gain[c]).astype(bf16)
            for i in range(3):
                t = dot(n, w[i, c * width:(c + 1) * width, :])
                acc[i] = t if c == 0 else acc[i] + t
        q, k, v = (t.astype(bf16) for t in acc)
        return inv, q, k, v

    head_of = lax.broadcasted_iota(jnp.int32, (1, width), 1) // HEAD_DIM

    def only(h, t):
        return jnp.where(head_of == h, t, jnp.zeros_like(t))

    def attend(q, k, v, allowed, saved):
        out = None
        for h in range(heads):
            s = dot_nt(only(h, q), k) * HEAD_DIM ** (-0.5)
            s = jnp.where(allowed, s, neg_fill)
            e = jnp.exp(s - jnp.max(s, axis=-1, keepdims=True))
            p = e * (1.0 / jnp.sum(e, axis=-1, keepdims=True))
            saved[h] = p
            t = dot(p.astype(bf16), only(h, v))
            out = t if h == 0 else out + t
        return out.astype(bf16)

    def back(x, dx, inv, gain, w, wo, q, k, v, saved, dn):
        da = None
        for c in range(groups):
            t = dot_nt(dx[c], wo[:, c * width:(c + 1) * width])
            da = t if c == 0 else da + t
        da = da.astype(bf16)
        dq = dk = dv = None
        for h in range(heads):
            dah = only(h, da)
            p = saved[h]
            dp = dot_nt(dah, v)
            tv = dot_tn(p.astype(bf16), dah)
            ds = p * (dp - jnp.sum(dp * p, axis=-1, keepdims=True))
            ds = (ds * HEAD_DIM ** (-0.5)).astype(bf16)
            tq = dot(ds, only(h, k))
            tk = dot_tn(ds, only(h, q))
            dq, dk, dv = (tq, tk, tv) if h == 0 else (dq + tq, dk + tk, dv + tv)
        dq, dk, dv = dq.astype(bf16), dk.astype(bf16), dv.astype(bf16)
        total = jnp.zeros((x.shape[1], 1), f32)
        for c in range(groups):
            at = slice(c * width, (c + 1) * width)
            g = dot_nt(dq, w[0, at, :]) + dot_nt(dk, w[1, at, :]) + dot_nt(dv, w[2, at, :])
            g = g.astype(bf16)
            dn[c] = g
            total = total + jnp.sum(x[c].astype(f32) * (g.astype(f32) * gain[c]), axis=-1, keepdims=True)
        slope = inv * inv * inv * total * (1.0 / features)

        def part(c):
            return inv * (dn[c].astype(f32) * gain[c]) - x[c].astype(f32) * slope

        return part

    cells_out = spread_start(xr, 0)

    down = lax.broadcasted_iota(jnp.int32, (rows, rows), 0)
    over = lax.broadcasted_iota(jnp.int32, (rows, rows), 1)

    def pair(ref):
        along = jnp.broadcast_to(ref[...].astype(f32), (rows, rows))
        return along, along.T

    to_over, to_down = pair(dest)
    same = to_over == to_down
    rank_over = jnp.sum(jnp.where(same & (down < over), 1.0, 0.0), axis=0, keepdims=True)
    slot_over = to_over[0:1, :] * cap + rank_over
    at_slot = lax.broadcasted_iota(jnp.int32, (slots, rows), 0).astype(f32)
    place = jnp.where(at_slot == slot_over, 1.0, 0.0).astype(bf16)
    _, key_down = pair(key)
    lane = lax.broadcasted_iota(jnp.int32, (rows, KEY_LANES), 1).astype(f32)
    marks = jnp.where(key_down[:, :KEY_LANES] == lane, 1.0, 0.0).astype(bf16)
    e_out[...] = dot(place, marks).astype(bf16)
    d_out_buf[...] = dot(place, d_result[...]).astype(bf16)
    early = exchange_start(d_out_buf, inner_chunk(dxc), 0)
    early_keys = exchange_start(e_out, chunk(e_in), 1)

    cells_out = spread_relay(xr, 0, cells_out)
    seg_over, seg_down = pair(seg)
    row_allowed = (seg_over == seg_down) & (down // TILE == over // TILE)
    spread_wait(cells_out)

    loads[0].wait()
    row_inv, rq, rk, rv = project(xr, row_gain, rw)
    exchange_wait(early)
    exchange_wait(early_keys)
    d_spread = spread_start(dxc, 1)
    row_att = attend(rq, rk, rv, row_allowed, p_row)
    loads[1].wait()

    def row_term(c):
        return dot(row_att, ro[:, lanes(c)])

    bufs = (r_sib, r_got, r_x, r_xgot)
    state = sum_start(row_term, bufs, 0)
    d_spread = spread_relay(dxc, 1, d_spread)
    state = sum_cross(bufs, 0, state)
    mixed = (cells[...].astype(f32) + sum_end(row_term, bufs, state)).astype(bf16)
    m_out[...] = dot(place, mixed).astype(bf16)
    arriving = exchange_start(m_out, inner_chunk(xc), 2)

    marks_in = e_in[...]
    col_allowed = dot_nt(marks_in, marks_in) > 0.5
    col_allowed = col_allowed | (
        lax.broadcasted_iota(jnp.int32, (slots, slots), 0)
        == lax.broadcasted_iota(jnp.int32, (slots, slots), 1)
    )
    loads[2].wait()
    loads[3].wait()
    exchange_wait(arriving)
    col_spread = spread_start(xc, 2)
    spread_wait(d_spread)
    spread_wait(spread_relay(xc, 2, col_spread))

    col_inv, cq, ck, cv = project(xc, col_gain, cw)
    col_att = attend(cq, ck, cv, col_allowed, p_col)

    def col_term(c):
        return dot(col_att, co[:, lanes(c)])

    fwd_bufs = (c_sib, c_got, c_x, c_xgot)
    fwd = sum_start(col_term, fwd_bufs, 1)
    fwd = sum_cross(fwd_bufs, 1, fwd)
    col_part = back(xc, dxc, col_inv, col_gain, cw, co, cq, ck, cv, p_col, dn_col)
    bwd_bufs = (b_sib, b_got, b_x, b_xgot)
    bwd = sum_start(col_part, bwd_bufs, 2)
    bwd = sum_cross(bwd_bufs, 2, bwd)
    g_out[...] = (dxc[me].astype(f32) + sum_end(col_part, bwd_bufs, bwd)).astype(bf16)
    g_copies = exchange_start(g_out, chunk(g_back), 3)
    s_out[...] = (xc[me].astype(f32) + sum_end(col_term, fwd_bufs, fwd)).astype(bf16)
    s_copies = exchange_start(s_out, chunk(s_back), 4)
    exchange_wait(g_copies)
    dxr[me] = dot_tn(place, g_back[...]).astype(bf16)
    last = spread_start(dxr, 3)
    exchange_wait(s_copies)
    result[...] = dot_tn(place, s_back[...]).astype(bf16)
    spread_wait(spread_relay(dxr, 3, last))

    row_part = back(xr, dxr, row_inv, row_gain, rw, ro, rq, rk, rv, p_row, dn_row)
    end_bufs = (q_sib, q_got, q_x, q_xgot)
    end = sum_start(row_part, end_bufs, 3)
    end = sum_cross(end_bufs, 3, end)
    d_cells[...] = (dxr[me].astype(f32) + sum_end(row_part, end_bufs, end)).astype(bf16)
    for copy in pending:
        copy.wait_send()


def fused(bands, cells, row_gain, row_qkv, row_out, col_gain, col_qkv, col_out, row_seg, col_dest, index, d_result):
    rows, width = cells.shape
    features = row_out.shape[1]
    groups = features // width
    heads = width // HEAD_DIM
    cap = 3 * rows // (2 * bands)
    slots = bands * cap
    vmem = pl.BlockSpec(memory_space=pltpu.VMEM)
    hbm = pl.BlockSpec(memory_space=pl.ANY)

    def sum_bufs(n):
        return [
            pltpu.VMEM((2, n, width), bf16), pltpu.VMEM((2, n, width), bf16),
            pltpu.VMEM((n, width), bf16), pltpu.VMEM((n, width), bf16),
        ]

    return pl.pallas_call(
        functools.partial(fused_kernel, bands, cap),
        out_shape=(
            jax.ShapeDtypeStruct(cells.shape, bf16),
            jax.ShapeDtypeStruct(cells.shape, bf16),
        ),
        in_specs=[vmem] * 7 + [hbm] * 4,
        out_specs=(vmem, vmem),
        scratch_shapes=[
            pltpu.VMEM(row_qkv.shape, bf16), pltpu.VMEM(row_out.shape, bf16),
            pltpu.VMEM(col_qkv.shape, bf16), pltpu.VMEM(col_out.shape, bf16),
            pltpu.VMEM((groups, rows, width), bf16), pltpu.VMEM((groups, slots, width), bf16),
            pltpu.VMEM((groups, slots, width), bf16), pltpu.VMEM((groups, rows, width), bf16),
            pltpu.VMEM((slots, KEY_LANES), bf16), pltpu.VMEM((slots, KEY_LANES), bf16),
            *[pltpu.VMEM((slots, width), bf16) for _ in range(6)],
            *sum_bufs(rows), *sum_bufs(slots), *sum_bufs(slots), *sum_bufs(rows),
            pltpu.VMEM((heads, rows, rows), f32), pltpu.VMEM((heads, slots, slots), f32),
            pltpu.VMEM((groups, rows, width), bf16), pltpu.VMEM((groups, slots, width), bf16),
            pltpu.SemaphoreType.DMA((4,)),
            pltpu.SemaphoreType.DMA((4, 3)), pltpu.SemaphoreType.DMA((4, 3)),
            pltpu.SemaphoreType.DMA((4, 3)), pltpu.SemaphoreType.DMA((4, 3)),
            pltpu.SemaphoreType.DMA((5, bands)), pltpu.SemaphoreType.DMA((5, bands)),
        ],
        compiler_params=pltpu.CompilerParams(
            collective_id=0, has_side_effects=True, vmem_limit_bytes=48 * 1024 * 1024
        ),
        cost_estimate=pl.CostEstimate(flops=8 * 10**9, bytes_accessed=5 * 10**6, transcendentals=10**6),
    )(
        cells, d_result,
        row_gain.reshape(groups, 1, width), col_gain.reshape(groups, 1, width),
        row_seg.reshape(1, rows), col_dest.reshape(1, rows), index.reshape(1, rows),
        row_qkv, row_out, col_qkv, col_out,
    )


def block_terms(inputs, norm_gain, query_key_value_weight, w_out, allowed, tile_rows):
    values = inputs.astype(jnp.float32)
    inv_rms = lax.rsqrt(jnp.mean(values * values, axis=-1, keepdims=True) + norm_eps)
    normalized_cells = (values * inv_rms * norm_gain).astype(jnp.bfloat16)
    projected_heads = jnp.einsum(
        "lu,xuh->xlh", normalized_cells, query_key_value_weight, preferred_element_type=jnp.float32
    ).astype(jnp.bfloat16)
    row_count = inputs.shape[0]
    feat_width = query_key_value_weight.shape[2]
    head_count = feat_width // HEAD_DIM
    shaped = projected_heads.reshape(3, row_count // tile_rows, tile_rows, head_count, HEAD_DIM)
    scores = jnp.einsum(
        "bqhe,bkhe->bhqk", shaped[0], shaped[1], preferred_element_type=jnp.float32
    ) * HEAD_DIM ** (-0.5)
    scores = jnp.where(allowed[:, None], scores, neg_fill)
    scores = scores - lax.stop_gradient(jnp.max(scores, axis=-1, keepdims=True))
    expd = jnp.exp(scores)
    attn_probs = (expd / jnp.sum(expd, axis=-1, keepdims=True)).astype(jnp.bfloat16)
    attended = jnp.einsum(
        "bhqk,bkhe->bqhe", attn_probs, shaped[2], preferred_element_type=jnp.float32
    ).astype(jnp.bfloat16)
    attended = attended.reshape(row_count, feat_width)
    return jnp.dot(attended, w_out, preferred_element_type=jnp.float32)


def column_band_mask(col_keys):
    positions = jnp.arange(col_keys.shape[0])
    same_col = (col_keys[:, None] == col_keys[None, :]) & (col_keys[None, :] > 0)
    return (same_col | (positions[:, None] == positions[None, :]))[None]


def widen(block):
    return lax.all_gather(block, "mp", axis=1, tiled=True)


def narrow(terms):
    return lax.psum_scatter(
        terms.astype(jnp.bfloat16), "mp", scatter_dimension=1, tiled=True
    ).astype(jnp.float32)


def move_rows(rows):
    return lax.all_to_all(rows, "band", split_axis=0, concat_axis=0, tiled=True)


def on_device(
    cells,
    row_gain,
    row_qkv,
    row_out,
    col_gain,
    col_qkv,
    col_out,
    row_seg,
    col_dest,
    sheet_column_index,
    d_result,
):
    cell_rows, feat_width = cells.shape
    band_count = lax.axis_size("band")
    capacity = max(2, 3 * cell_rows // (2 * band_count))
    slot_total = band_count * capacity
    spare = (3 * cell_rows) % (2 * band_count) or capacity % 16
    if lax.axis_size("mp") == 4 and cell_rows == 2 * TILE and not spare:
        return fused(
            band_count, cells, row_gain, row_qkv, row_out, col_gain, col_qkv, col_out,
            row_seg, col_dest, sheet_column_index, d_result,
        )
    gathered = widen(cells)
    row_groups = row_seg.reshape(cell_rows // TILE, TILE)
    row_mask = row_groups[:, :, None] == row_groups[:, None, :]

    def row_local(inputs):
        return block_terms(inputs, row_gain, row_qkv, row_out, row_mask, TILE)

    row_terms, row_pull = jax.vjp(row_local, gathered)
    target = col_dest[:, 0]
    place = jnp.arange(cell_rows, dtype=jnp.int32)
    earlier = (target[:, None] == target[None, :]) & (place[None, :] < place[:, None])
    ranking = jnp.sum(earlier.astype(jnp.int32), axis=1)
    slot_index = target * capacity + ranking
    keys_out = (
        jnp.zeros((slot_total,), jnp.bfloat16)
        .at[slot_index]
        .set(sheet_column_index.astype(jnp.bfloat16))
    )
    back_in = jnp.zeros((slot_total, feat_width), jnp.bfloat16).at[slot_index].set(d_result)
    mixed_rows = (cells.astype(jnp.float32) + narrow(row_terms)).astype(jnp.bfloat16)
    outgoing = jnp.zeros((slot_total, feat_width), jnp.bfloat16).at[slot_index].set(mixed_rows)
    arrived, col_keys = (
        lax.all_to_all(outgoing, "band", split_axis=0, concat_axis=0, tiled=True),
        lax.all_to_all(keys_out, "band", split_axis=0, concat_axis=0, tiled=True),
    )
    column_full = widen(arrived)
    col_allowed = column_band_mask(col_keys)

    def col_local(inputs):
        return block_terms(inputs, col_gain, col_qkv, col_out, col_allowed, inputs.shape[0])

    col_terms, col_pull = jax.vjp(col_local, column_full)
    settled = (arrived.astype(jnp.float32) + narrow(col_terms)).astype(jnp.bfloat16)
    result = move_rows(settled)[slot_index]
    d_column = move_rows(back_in)
    (d_col_part,) = col_pull(widen(d_column).astype(jnp.float32))
    d_mixed_col = (d_column.astype(jnp.float32) + narrow(d_col_part.astype(jnp.float32))).astype(
        jnp.bfloat16
    )
    d_mixed = move_rows(d_mixed_col)[slot_index]
    (d_row_part,) = row_pull(widen(d_mixed).astype(jnp.float32))
    d_cells = (d_mixed.astype(jnp.float32) + narrow(d_row_part.astype(jnp.float32))).astype(
        jnp.bfloat16
    )
    return (result, d_cells)


def solution(mesh):
    in_specs = (
        P("band", "mp"),
        P(),
        P(None, None, "mp"),
        P("mp", None),
        P(),
        P(None, None, "mp"),
        P("mp", None),
        P("band"),
        P("band", None),
        P("band"),
        P("band", "mp"),
    )
    out_specs = (P("band", "mp"), P("band", "mp"))
    return jax.shard_map(
        on_device, mesh=mesh, in_specs=in_specs, out_specs=out_specs, check_vma=False
    )
```

```python
import functools

import jax
import jax.numpy as jnp
from jax import lax
from jax.experimental import pallas as pl
from jax.experimental.pallas import tpu as pltpu
from jax.sharding import PartitionSpec as P

HEAD_DIM = 64
TILE = 128


norm_eps = 1e-06
neg_fill = -1e30

MESH = pl.DeviceIdType.MESH
KEY_LANES = 128
f32, bf16 = jnp.float32, jnp.bfloat16


def dot(a, b):
    return lax.dot_general(a, b, (((1,), (0,)), ((), ())), preferred_element_type=f32)


def dot_nt(a, b):
    return lax.dot_general(a, b, (((1,), (1,)), ((), ())), preferred_element_type=f32)


def dot_tn(a, b):
    return lax.dot_general(a, b, (((0,), (0,)), ((), ())), preferred_element_type=f32)


def fused_kernel(
    bands, cap,
    cells, d_any, rg_any, cg_any, seg_any, dest_any, key_any, rw_any, ro_any, cw_any, co_any,
    result, d_cells,
    d_result, row_gain, col_gain, seg, dest, key, rw, ro, cw, co, xr, xc, dxc, dxr, e_out, e_in,
    d_out_buf, m_out, s_out, g_out, s_back, g_back,
    r_sib, r_got, r_x, r_xgot, c_sib, c_got, c_x, c_xgot,
    b_sib, b_got, b_x, b_xgot, q_sib, q_got, q_x, q_xgot,
    p_row, p_col, dn_row, dn_col,
    w_sem, fw_send, fw_recv, ag_send, ag_recv, rs_send, rs_recv, aa_send, aa_recv,
):
    rows, width = cells.shape
    groups = xr.shape[0]
    slots = bands * cap
    heads = width // HEAD_DIM
    features = groups * width
    band, me = lax.axis_index("band"), lax.axis_index("mp")
    near = me + 1 - 2 * lax.rem(me, 2)
    far = lax.rem(me + 2, 4)
    corner = lax.rem(near + 2, 4)
    pending = []

    loads = []
    for i, (src, dst) in enumerate((
        (cells, xr.at[me]), (dest_any, dest), (key_any, key), (d_any, d_result), (seg_any, seg),
        (rg_any, row_gain), (rw_any, rw), (ro_any, ro), (cg_any, col_gain), (cw_any, cw), (co_any, co),
    )):
        load = pltpu.make_async_copy(src, dst, w_sem.at[i])
        load.start()
        loads.append(load)

    barrier = pltpu.get_barrier_semaphore()
    for peer in (near, far):
        pl.semaphore_signal(barrier, inc=1, device_id=(band, peer), device_id_type=MESH)
    for d in range(1, bands):
        pl.semaphore_signal(
            barrier, inc=1, device_id=(lax.rem(band + d, bands), me), device_id_type=MESH
        )
    pl.semaphore_wait(barrier, bands + 1)

    def send(src, dst, send_sem, recv_sem, to):
        copy = pltpu.make_async_remote_copy(
            src_ref=src, dst_ref=dst, send_sem=send_sem, recv_sem=recv_sem,
            device_id=to, device_id_type=MESH,
        )
        copy.start()
        pending.append(copy)
        return copy

    def spread_start(buf, n):
        across = send(buf.at[me], buf.at[me], ag_send.at[n, 0], ag_recv.at[n, 0], (band, far))
        beside = send(buf.at[me], buf.at[me], ag_send.at[n, 1], ag_recv.at[n, 1], (band, near))
        return across, beside

    def spread_relay(buf, n, started):
        across, beside = started
        across.wait_recv()
        relay = send(buf.at[far], buf.at[far], ag_send.at[n, 2], ag_recv.at[n, 2], (band, near))
        return beside, relay

    def spread_wait(copies):
        for copy in copies:
            copy.wait_recv()

    def exchange_start(src, dst_at, n):
        copies = []
        for d in range(1, bands):
            to = lax.rem(band + d, bands)
            copies.append(
                send(src.at[pl.ds(pl.multiple_of(to * cap, 16), cap)], dst_at(band),
                     aa_send.at[n, d], aa_recv.at[n, d], (to, me))
            )
        dst_at(band)[...] = src[pl.ds(pl.multiple_of(band * cap, 16), cap), :]
        return copies

    def exchange_wait(copies):
        for copy in copies:
            copy.wait_recv()

    def chunk(ref):
        return lambda s: ref.at[pl.ds(pl.multiple_of(s * cap, 16), cap)]

    def inner_chunk(ref):
        return lambda s: ref.at[me, pl.ds(pl.multiple_of(s * cap, 16), cap)]

    def sum_start(part, bufs, n):
        sib, got, out, arrived = bufs
        sib[0] = part(corner).astype(bf16)
        a = send(sib.at[0], got.at[0], rs_send.at[n, 0], rs_recv.at[n, 0], (band, near))
        mine = part(far)
        a.wait_recv()
        out[...] = (mine + got[0].astype(f32)).astype(bf16)
        c = send(out, arrived, rs_send.at[n, 2], rs_recv.at[n, 2], (band, far))
        sib[1] = part(near).astype(bf16)
        b = send(sib.at[1], got.at[1], rs_send.at[n, 1], rs_recv.at[n, 1], (band, near))
        return b, c

    def sum_end(part, bufs, state):
        _, got, _, arrived = bufs
        b, c = state
        own = part(me).astype(bf16).astype(f32)
        b.wait_recv()
        own = own + got[1].astype(f32)
        c.wait_recv()
        return own + arrived[...].astype(f32)

    def lanes(c):
        return pl.ds(pl.multiple_of(c * width, 128), width)

    def project(x, gain, w):
        total = jnp.zeros((x.shape[1], 1), f32)
        for c in range(groups):
            v = x[c].astype(f32)
            total = total + jnp.sum(v * v, axis=-1, keepdims=True)
        inv = lax.rsqrt(total / features + norm_eps)
        acc = [None] * 3
        for c in range(groups):
            n = (x[c].astype(f32) * inv * gain[c]).astype(bf16)
            for i in range(3):
                t = dot(n, w[i, c * width:(c + 1) * width, :])
                acc[i] = t if c == 0 else acc[i] + t
        q, k, v = (t.astype(bf16) for t in acc)
        return inv, q, k, v

    head_of = lax.broadcasted_iota(jnp.int32, (1, width), 1) // HEAD_DIM

    def only(h, t):
        return jnp.where(head_of == h, t, jnp.zeros_like(t))

    def attend(q, k, v, allowed, saved):
        out = None
        for h in range(heads):
            s = dot_nt(only(h, q), k) * HEAD_DIM ** (-0.5)
            s = jnp.where(allowed, s, neg_fill)
            e = jnp.exp(s - jnp.max(s, axis=-1, keepdims=True))
            p = e * (1.0 / jnp.sum(e, axis=-1, keepdims=True))
            saved[h] = p
            t = dot(p.astype(bf16), only(h, v))
            out = t if h == 0 else out + t
        return out.astype(bf16)

    def back(x, dx, inv, gain, w, wo, q, k, v, saved, dn):
        da = None
        for c in range(groups):
            t = dot_nt(dx[c], wo[:, c * width:(c + 1) * width])
            da = t if c == 0 else da + t
        da = da.astype(bf16)
        dq = dk = dv = None
        for h in range(heads):
            dah = only(h, da)
            p = saved[h]
            dp = dot_nt(dah, v)
            tv = dot_tn(p.astype(bf16), dah)
            ds = p * (dp - jnp.sum(dp * p, axis=-1, keepdims=True))
            ds = (ds * HEAD_DIM ** (-0.5)).astype(bf16)
            tq = dot(ds, only(h, k))
            tk = dot_tn(ds, only(h, q))
            dq, dk, dv = (tq, tk, tv) if h == 0 else (dq + tq, dk + tk, dv + tv)
        dq, dk, dv = dq.astype(bf16), dk.astype(bf16), dv.astype(bf16)
        total = jnp.zeros((x.shape[1], 1), f32)
        for c in range(groups):
            at = slice(c * width, (c + 1) * width)
            g = dot_nt(dq, w[0, at, :]) + dot_nt(dk, w[1, at, :]) + dot_nt(dv, w[2, at, :])
            g = g.astype(bf16)
            dn[c] = g
            total = total + jnp.sum(x[c].astype(f32) * (g.astype(f32) * gain[c]), axis=-1, keepdims=True)
        slope = inv * inv * inv * total * (1.0 / features)

        def part(c):
            return inv * (dn[c].astype(f32) * gain[c]) - x[c].astype(f32) * slope

        return part

    loads[0].wait()
    cells_out = spread_start(xr, 0)

    down = lax.broadcasted_iota(jnp.int32, (rows, rows), 0)
    over = lax.broadcasted_iota(jnp.int32, (rows, rows), 1)

    def pair(ref):
        along = jnp.broadcast_to(ref[...].astype(f32), (rows, rows))
        return along, along.T

    for i in (1, 2, 3, 4):
        loads[i].wait()
    to_over, to_down = pair(dest)
    same = to_over == to_down
    rank_over = jnp.sum(jnp.where(same & (down < over), 1.0, 0.0), axis=0, keepdims=True)
    slot_over = to_over[0:1, :] * cap + rank_over
    at_slot = lax.broadcasted_iota(jnp.int32, (slots, rows), 0).astype(f32)
    place = jnp.where(at_slot == slot_over, 1.0, 0.0).astype(bf16)
    _, key_down = pair(key)
    lane = lax.broadcasted_iota(jnp.int32, (rows, KEY_LANES), 1).astype(f32)
    marks = jnp.where(key_down[:, :KEY_LANES] == lane, 1.0, 0.0).astype(bf16)
    e_out[...] = dot(place, marks).astype(bf16)
    d_out_buf[...] = dot(place, d_result[...]).astype(bf16)
    early = exchange_start(d_out_buf, inner_chunk(dxc), 0)
    early_keys = exchange_start(e_out, chunk(e_in), 1)

    cells_out = spread_relay(xr, 0, cells_out)
    seg_over, seg_down = pair(seg)
    row_allowed = (seg_over == seg_down) & (down // TILE == over // TILE)
    spread_wait(cells_out)

    loads[5].wait()
    loads[6].wait()
    row_inv, rq, rk, rv = project(xr, row_gain, rw)
    exchange_wait(early)
    exchange_wait(early_keys)
    d_spread = spread_start(dxc, 1)
    row_att = attend(rq, rk, rv, row_allowed, p_row)
    loads[7].wait()

    def row_term(c):
        return dot(row_att, ro[:, lanes(c)])

    bufs = (r_sib, r_got, r_x, r_xgot)
    state = sum_start(row_term, bufs, 0)
    d_spread = spread_relay(dxc, 1, d_spread)
    mixed = (xr[me].astype(f32) + sum_end(row_term, bufs, state)).astype(bf16)
    m_out[...] = dot(place, mixed).astype(bf16)
    arriving = exchange_start(m_out, inner_chunk(xc), 2)

    marks_in = e_in[...]
    col_allowed = dot_nt(marks_in, marks_in) > 0.5
    col_allowed = col_allowed | (
        lax.broadcasted_iota(jnp.int32, (slots, slots), 0)
        == lax.broadcasted_iota(jnp.int32, (slots, slots), 1)
    )
    for i in (8, 9, 10):
        loads[i].wait()
    moved = []
    for d in range(bands):
        if d:
            arriving[d - 1].wait_recv()
        at = pl.ds(pl.multiple_of(lax.rem(band + bands - d, bands) * cap, 16), cap)
        mine = xc.at[me, at]
        across = send(mine, mine, fw_send.at[d, 0], fw_recv.at[d, 0], (band, far))
        beside = send(mine, mine, fw_send.at[d, 1], fw_recv.at[d, 1], (band, near))
        moved.append((at, across, beside))
    spread_wait(d_spread)
    relays = []
    for d, (at, across, _) in enumerate(moved):
        across.wait_recv()
        theirs = xc.at[far, at]
        relays.append(send(theirs, theirs, fw_send.at[d, 2], fw_recv.at[d, 2], (band, near)))
    for _, _, beside in moved:
        beside.wait_recv()
    spread_wait(relays)

    col_inv, cq, ck, cv = project(xc, col_gain, cw)
    col_att = attend(cq, ck, cv, col_allowed, p_col)

    def col_term(c):
        return dot(col_att, co[:, lanes(c)])

    fwd_bufs = (c_sib, c_got, c_x, c_xgot)
    fwd = sum_start(col_term, fwd_bufs, 1)
    col_part = back(xc, dxc, col_inv, col_gain, cw, co, cq, ck, cv, p_col, dn_col)
    bwd_bufs = (b_sib, b_got, b_x, b_xgot)
    bwd = sum_start(col_part, bwd_bufs, 2)
    g_out[...] = (dxc[me].astype(f32) + sum_end(col_part, bwd_bufs, bwd)).astype(bf16)
    g_copies = exchange_start(g_out, chunk(g_back), 3)
    s_out[...] = (xc[me].astype(f32) + sum_end(col_term, fwd_bufs, fwd)).astype(bf16)
    s_copies = exchange_start(s_out, chunk(s_back), 4)
    exchange_wait(g_copies)
    dxr[me] = dot_tn(place, g_back[...]).astype(bf16)
    last = spread_start(dxr, 3)
    exchange_wait(s_copies)
    result[...] = dot_tn(place, s_back[...]).astype(bf16)
    spread_wait(spread_relay(dxr, 3, last))

    row_part = back(xr, dxr, row_inv, row_gain, rw, ro, rq, rk, rv, p_row, dn_row)
    end_bufs = (q_sib, q_got, q_x, q_xgot)
    end = sum_start(row_part, end_bufs, 3)
    d_cells[...] = (dxr[me].astype(f32) + sum_end(row_part, end_bufs, end)).astype(bf16)
    for copy in pending:
        copy.wait_send()


def fused(bands, cells, row_gain, row_qkv, row_out, col_gain, col_qkv, col_out, row_seg, col_dest, index, d_result):
    rows, width = cells.shape
    features = row_out.shape[1]
    groups = features // width
    heads = width // HEAD_DIM
    cap = 3 * rows // (2 * bands)
    slots = bands * cap
    vmem = pl.BlockSpec(memory_space=pltpu.VMEM)
    hbm = pl.BlockSpec(memory_space=pltpu.HBM)

    def sum_bufs(n):
        return [
            pltpu.VMEM((2, n, width), bf16), pltpu.VMEM((2, n, width), bf16),
            pltpu.VMEM((n, width), bf16), pltpu.VMEM((n, width), bf16),
        ]

    return pl.pallas_call(
        functools.partial(fused_kernel, bands, cap),
        out_shape=(
            jax.ShapeDtypeStruct(cells.shape, bf16),
            jax.ShapeDtypeStruct(cells.shape, bf16),
        ),
        in_specs=[hbm] * 11,
        out_specs=(vmem, vmem),
        scratch_shapes=[
            pltpu.VMEM(d_result.shape, bf16),
            pltpu.VMEM((groups, 1, width), f32), pltpu.VMEM((groups, 1, width), f32),
            *[pltpu.VMEM((1, rows), jnp.int32) for _ in range(3)],
            pltpu.VMEM(row_qkv.shape, bf16), pltpu.VMEM(row_out.shape, bf16),
            pltpu.VMEM(col_qkv.shape, bf16), pltpu.VMEM(col_out.shape, bf16),
            pltpu.VMEM((groups, rows, width), bf16), pltpu.VMEM((groups, slots, width), bf16),
            pltpu.VMEM((groups, slots, width), bf16), pltpu.VMEM((groups, rows, width), bf16),
            pltpu.VMEM((slots, KEY_LANES), bf16), pltpu.VMEM((slots, KEY_LANES), bf16),
            *[pltpu.VMEM((slots, width), bf16) for _ in range(6)],
            *sum_bufs(rows), *sum_bufs(slots), *sum_bufs(slots), *sum_bufs(rows),
            pltpu.VMEM((heads, rows, rows), f32), pltpu.VMEM((heads, slots, slots), f32),
            pltpu.VMEM((groups, rows, width), bf16), pltpu.VMEM((groups, slots, width), bf16),
            pltpu.SemaphoreType.DMA((11,)),
            pltpu.SemaphoreType.DMA((bands, 3)), pltpu.SemaphoreType.DMA((bands, 3)),
            pltpu.SemaphoreType.DMA((4, 3)), pltpu.SemaphoreType.DMA((4, 3)),
            pltpu.SemaphoreType.DMA((4, 3)), pltpu.SemaphoreType.DMA((4, 3)),
            pltpu.SemaphoreType.DMA((5, bands)), pltpu.SemaphoreType.DMA((5, bands)),
        ],
        compiler_params=pltpu.CompilerParams(
            collective_id=0, has_side_effects=True, vmem_limit_bytes=60 * 1024 * 1024
        ),
        cost_estimate=pl.CostEstimate(flops=8 * 10**9, bytes_accessed=5 * 10**6, transcendentals=10**6),
    )(
        cells, d_result,
        row_gain.reshape(groups, 1, width), col_gain.reshape(groups, 1, width),
        row_seg.reshape(1, rows), col_dest.reshape(1, rows), index.reshape(1, rows),
        row_qkv, row_out, col_qkv, col_out,
    )


def block_terms(inputs, norm_gain, query_key_value_weight, w_out, allowed, tile_rows):
    values = inputs.astype(jnp.float32)
    inv_rms = lax.rsqrt(jnp.mean(values * values, axis=-1, keepdims=True) + norm_eps)
    normalized_cells = (values * inv_rms * norm_gain).astype(jnp.bfloat16)
    projected_heads = jnp.einsum(
        "lu,xuh->xlh", normalized_cells, query_key_value_weight, preferred_element_type=jnp.float32
    ).astype(jnp.bfloat16)
    row_count = inputs.shape[0]
    feat_width = query_key_value_weight.shape[2]
    head_count = feat_width // HEAD_DIM
    shaped = projected_heads.reshape(3, row_count // tile_rows, tile_rows, head_count, HEAD_DIM)
    scores = jnp.einsum(
        "bqhe,bkhe->bhqk", shaped[0], shaped[1], preferred_element_type=jnp.float32
    ) * HEAD_DIM ** (-0.5)
    scores = jnp.where(allowed[:, None], scores, neg_fill)
    scores = scores - lax.stop_gradient(jnp.max(scores, axis=-1, keepdims=True))
    expd = jnp.exp(scores)
    attn_probs = (expd / jnp.sum(expd, axis=-1, keepdims=True)).astype(jnp.bfloat16)
    attended = jnp.einsum(
        "bhqk,bkhe->bqhe", attn_probs, shaped[2], preferred_element_type=jnp.float32
    ).astype(jnp.bfloat16)
    attended = attended.reshape(row_count, feat_width)
    return jnp.dot(attended, w_out, preferred_element_type=jnp.float32)


def column_band_mask(col_keys):
    positions = jnp.arange(col_keys.shape[0])
    same_col = (col_keys[:, None] == col_keys[None, :]) & (col_keys[None, :] > 0)
    return (same_col | (positions[:, None] == positions[None, :]))[None]


def widen(block):
    return lax.all_gather(block, "mp", axis=1, tiled=True)


def narrow(terms):
    return lax.psum_scatter(
        terms.astype(jnp.bfloat16), "mp", scatter_dimension=1, tiled=True
    ).astype(jnp.float32)


def move_rows(rows):
    return lax.all_to_all(rows, "band", split_axis=0, concat_axis=0, tiled=True)


def on_device(
    cells,
    row_gain,
    row_qkv,
    row_out,
    col_gain,
    col_qkv,
    col_out,
    row_seg,
    col_dest,
    sheet_column_index,
    d_result,
):
    cell_rows, feat_width = cells.shape
    band_count = lax.axis_size("band")
    capacity = max(2, 3 * cell_rows // (2 * band_count))
    slot_total = band_count * capacity
    spare = (3 * cell_rows) % (2 * band_count) or capacity % 16
    if lax.axis_size("mp") == 4 and cell_rows == 2 * TILE and not spare:
        return fused(
            band_count, cells, row_gain, row_qkv, row_out, col_gain, col_qkv, col_out,
            row_seg, col_dest, sheet_column_index, d_result,
        )
    gathered = widen(cells)
    row_groups = row_seg.reshape(cell_rows // TILE, TILE)
    row_mask = row_groups[:, :, None] == row_groups[:, None, :]

    def row_local(inputs):
        return block_terms(inputs, row_gain, row_qkv, row_out, row_mask, TILE)

    row_terms, row_pull = jax.vjp(row_local, gathered)
    target = col_dest[:, 0]
    place = jnp.arange(cell_rows, dtype=jnp.int32)
    earlier = (target[:, None] == target[None, :]) & (place[None, :] < place[:, None])
    ranking = jnp.sum(earlier.astype(jnp.int32), axis=1)
    slot_index = target * capacity + ranking
    keys_out = (
        jnp.zeros((slot_total,), jnp.bfloat16)
        .at[slot_index]
        .set(sheet_column_index.astype(jnp.bfloat16))
    )
    back_in = jnp.zeros((slot_total, feat_width), jnp.bfloat16).at[slot_index].set(d_result)
    mixed_rows = (cells.astype(jnp.float32) + narrow(row_terms)).astype(jnp.bfloat16)
    outgoing = jnp.zeros((slot_total, feat_width), jnp.bfloat16).at[slot_index].set(mixed_rows)
    arrived, col_keys = (
        lax.all_to_all(outgoing, "band", split_axis=0, concat_axis=0, tiled=True),
        lax.all_to_all(keys_out, "band", split_axis=0, concat_axis=0, tiled=True),
    )
    column_full = widen(arrived)
    col_allowed = column_band_mask(col_keys)

    def col_local(inputs):
        return block_terms(inputs, col_gain, col_qkv, col_out, col_allowed, inputs.shape[0])

    col_terms, col_pull = jax.vjp(col_local, column_full)
    settled = (arrived.astype(jnp.float32) + narrow(col_terms)).astype(jnp.bfloat16)
    result = move_rows(settled)[slot_index]
    d_column = move_rows(back_in)
    (d_col_part,) = col_pull(widen(d_column).astype(jnp.float32))
    d_mixed_col = (d_column.astype(jnp.float32) + narrow(d_col_part.astype(jnp.float32))).astype(
        jnp.bfloat16
    )
    d_mixed = move_rows(d_mixed_col)[slot_index]
    (d_row_part,) = row_pull(widen(d_mixed).astype(jnp.float32))
    d_cells = (d_mixed.astype(jnp.float32) + narrow(d_row_part.astype(jnp.float32))).astype(
        jnp.bfloat16
    )
    return (result, d_cells)


def solution(mesh):
    in_specs = (
        P("band", "mp"),
        P(),
        P(None, None, "mp"),
        P("mp", None),
        P(),
        P(None, None, "mp"),
        P("mp", None),
        P("band"),
        P("band", None),
        P("band"),
        P("band", "mp"),
    )
    out_specs = (P("band", "mp"), P("band", "mp"))
    return jax.shard_map(
        on_device, mesh=mesh, in_specs=in_specs, out_specs=out_specs, check_vma=False
    )
```

```python
import functools

import jax
import jax.numpy as jnp
from jax import lax
from jax.experimental import pallas as pl
from jax.experimental.pallas import tpu as pltpu
from jax.sharding import PartitionSpec as P

HEAD_DIM = 64
TILE = 128


norm_eps = 1e-06
neg_fill = -1e30

MESH = pl.DeviceIdType.MESH
KEY_LANES = 128
f32, bf16 = jnp.float32, jnp.bfloat16


def dot(a, b):
    return lax.dot_general(a, b, (((1,), (0,)), ((), ())), preferred_element_type=f32)


def dot_nt(a, b):
    return lax.dot_general(a, b, (((1,), (1,)), ((), ())), preferred_element_type=f32)


def dot_tn(a, b):
    return lax.dot_general(a, b, (((0,), (0,)), ((), ())), preferred_element_type=f32)


def fused_kernel(
    bands, cap,
    cells, d_any, rg_any, cg_any, seg_any, dest_any, key_any, rw_any, ro_any, cw_any, co_any,
    result, d_cells,
    d_result, row_gain, col_gain, seg, dest, key, rw, ro, cw, co, xr, xc, dxc, dxr, e_out, e_in,
    d_out_buf, m_out, s_out, g_out, s_back, g_back,
    r_sib, r_got, r_x, r_xgot, c_sib, c_got, c_x, c_xgot,
    b_sib, b_got, b_x, b_xgot, q_sib, q_got, q_x, q_xgot,
    p_row, p_col, dn_row, dn_col,
    w_sem, fw_send, fw_recv, ag_send, ag_recv, rs_send, rs_recv, aa_send, aa_recv,
):
    rows, width = cells.shape
    groups = xr.shape[0]
    slots = bands * cap
    heads = width // HEAD_DIM
    features = groups * width
    band, me = lax.axis_index("band"), lax.axis_index("mp")
    near = me + 1 - 2 * lax.rem(me, 2)
    far = lax.rem(me + 2, 4)
    corner = lax.rem(near + 2, 4)
    pending = []

    loads = []
    for i, (src, dst) in enumerate((
        (cells, xr.at[me]), (dest_any, dest), (key_any, key), (d_any, d_result), (seg_any, seg),
        (rg_any, row_gain), (rw_any, rw), (ro_any, ro), (cg_any, col_gain), (cw_any, cw), (co_any, co),
    )):
        load = pltpu.make_async_copy(src, dst, w_sem.at[i])
        load.start()
        loads.append(load)

    barrier = pltpu.get_barrier_semaphore()
    for peer in (near, far):
        pl.semaphore_signal(barrier, inc=1, device_id=(band, peer), device_id_type=MESH)
    for d in range(1, bands):
        pl.semaphore_signal(
            barrier, inc=1, device_id=(lax.rem(band + d, bands), me), device_id_type=MESH
        )
    pl.semaphore_wait(barrier, bands + 1)

    def send(src, dst, send_sem, recv_sem, to):
        copy = pltpu.make_async_remote_copy(
            src_ref=src, dst_ref=dst, send_sem=send_sem, recv_sem=recv_sem,
            device_id=to, device_id_type=MESH,
        )
        copy.start()
        pending.append(copy)
        return copy

    def spread_start(buf, n):
        across = send(buf.at[me], buf.at[me], ag_send.at[n, 0], ag_recv.at[n, 0], (band, far))
        beside = send(buf.at[me], buf.at[me], ag_send.at[n, 1], ag_recv.at[n, 1], (band, near))
        return across, beside

    def spread_relay(buf, n, started):
        across, beside = started
        across.wait_recv()
        relay = send(buf.at[far], buf.at[far], ag_send.at[n, 2], ag_recv.at[n, 2], (band, near))
        return beside, relay

    def nothing():
        return None

    def arrival(buf, n, started):
        across, beside = started
        held = []

        def cross():
            held.append(spread_relay(buf, n, started)[1])

        def turn():
            held[0].wait_recv()

        return ((me, nothing), (near, beside.wait_recv), (far, cross), (corner, turn))

    def spread_wait(copies):
        for copy in copies:
            copy.wait_recv()

    def exchange_start(src, dst_at, n):
        copies = []
        for d in range(1, bands):
            to = lax.rem(band + d, bands)
            copies.append(
                send(src.at[pl.ds(pl.multiple_of(to * cap, 16), cap)], dst_at(band),
                     aa_send.at[n, d], aa_recv.at[n, d], (to, me))
            )
        dst_at(band)[...] = src[pl.ds(pl.multiple_of(band * cap, 16), cap), :]
        return copies

    def exchange_wait(copies):
        for copy in copies:
            copy.wait_recv()

    def chunk(ref):
        return lambda s: ref.at[pl.ds(pl.multiple_of(s * cap, 16), cap)]

    def inner_chunk(ref):
        return lambda s: ref.at[me, pl.ds(pl.multiple_of(s * cap, 16), cap)]

    def sum_start(part, bufs, n):
        return sum_cross(part, bufs, n, sum_open(part, bufs, n))

    def sum_open(part, bufs, n):
        sib, got, _, _ = bufs
        sib[0] = part(corner).astype(bf16)
        return send(sib.at[0], got.at[0], rs_send.at[n, 0], rs_recv.at[n, 0], (band, near))

    def sum_cross(part, bufs, n, a):
        sib, got, out, arrived = bufs
        mine = part(far)
        a.wait_recv()
        out[...] = (mine + got[0].astype(f32)).astype(bf16)
        c = send(out, arrived, rs_send.at[n, 2], rs_recv.at[n, 2], (band, far))
        sib[1] = part(near).astype(bf16)
        b = send(sib.at[1], got.at[1], rs_send.at[n, 1], rs_recv.at[n, 1], (band, near))
        return b, c

    def sum_end(part, bufs, state):
        _, got, _, arrived = bufs
        b, c = state
        own = part(me).astype(bf16).astype(f32)
        b.wait_recv()
        own = own + got[1].astype(f32)
        c.wait_recv()
        return own + arrived[...].astype(f32)

    def lanes(c):
        return pl.ds(pl.multiple_of(c * width, 128), width)

    def features_of(c):
        return pl.ds(pl.multiple_of(c * width, 128), width)

    def project(x, gain, w, order):
        total = jnp.zeros((x.shape[1], 1), f32)
        acc = [None] * 3
        for c, ready in order:
            ready()
            v = x[c].astype(f32)
            n = (v * gain[c]).astype(bf16)
            for i in range(3):
                t = dot(n, w[i, features_of(c), :])
                acc[i] = t if acc[i] is None else acc[i] + t
            total = total + jnp.sum(v * v, axis=-1, keepdims=True)
        inv = lax.rsqrt(total / features + norm_eps)
        q, k, v = ((t * inv).astype(bf16) for t in acc)
        return inv, q, k, v

    head_of = lax.broadcasted_iota(jnp.int32, (1, width), 1) // HEAD_DIM

    def only(h, t):
        return jnp.where(head_of == h, t, jnp.zeros_like(t))

    def attend(q, k, v, allowed, saved):
        out = None
        for h in range(heads):
            s = dot_nt(only(h, q), k) * HEAD_DIM ** (-0.5)
            s = jnp.where(allowed, s, neg_fill)
            e = jnp.exp(s - jnp.max(s, axis=-1, keepdims=True))
            p = e * (1.0 / jnp.sum(e, axis=-1, keepdims=True))
            saved[h] = p
            t = dot(p.astype(bf16), only(h, v))
            out = t if h == 0 else out + t
        return out.astype(bf16)

    def back(x, dx, inv, gain, w, wo, q, k, v, saved, dn, order, between):
        da = None
        for c, ready in order:
            ready()
            t = dot_nt(dx[c], wo[:, lanes(c)])
            da = t if da is None else da + t
        da = da.astype(bf16)
        dq = dk = dv = None
        for h in range(heads):
            dah = only(h, da)
            p = saved[h]
            dp = dot_nt(dah, v)
            tv = dot_tn(p.astype(bf16), dah)
            ds = p * (dp - jnp.sum(dp * p, axis=-1, keepdims=True))
            ds = (ds * HEAD_DIM ** (-0.5)).astype(bf16)
            tq = dot(ds, only(h, k))
            tk = dot_tn(ds, only(h, q))
            dq, dk, dv = (tq, tk, tv) if h == 0 else (dq + tq, dk + tk, dv + tv)
            if h == 1:
                between()
        dq, dk, dv = dq.astype(bf16), dk.astype(bf16), dv.astype(bf16)
        total = jnp.zeros((x.shape[1], 1), f32)
        for c in range(groups):
            at = slice(c * width, (c + 1) * width)
            g = dot_nt(dq, w[0, at, :]) + dot_nt(dk, w[1, at, :]) + dot_nt(dv, w[2, at, :])
            g = g.astype(bf16)
            dn[c] = g
            total = total + jnp.sum(x[c].astype(f32) * (g.astype(f32) * gain[c]), axis=-1, keepdims=True)
        slope = inv * inv * inv * total * (1.0 / features)

        def part(c):
            return inv * (dn[c].astype(f32) * gain[c]) - x[c].astype(f32) * slope

        return part

    loads[0].wait()
    cells_out = spread_start(xr, 0)

    down = lax.broadcasted_iota(jnp.int32, (rows, rows), 0)
    over = lax.broadcasted_iota(jnp.int32, (rows, rows), 1)

    def pair(ref):
        along = jnp.broadcast_to(ref[...].astype(f32), (rows, rows))
        return along, along.T

    for i in (1, 2, 3, 4):
        loads[i].wait()
    to_over, to_down = pair(dest)
    same = to_over == to_down
    rank_over = jnp.sum(jnp.where(same & (down < over), 1.0, 0.0), axis=0, keepdims=True)
    slot_over = to_over[0:1, :] * cap + rank_over
    at_slot = lax.broadcasted_iota(jnp.int32, (slots, rows), 0).astype(f32)
    place = jnp.where(at_slot == slot_over, 1.0, 0.0).astype(bf16)
    _, key_down = pair(key)
    lane = lax.broadcasted_iota(jnp.int32, (rows, KEY_LANES), 1).astype(f32)
    marks = jnp.where(key_down[:, :KEY_LANES] == lane, 1.0, 0.0).astype(bf16)
    e_out[...] = dot(place, marks).astype(bf16)
    d_out_buf[...] = dot(place, d_result[...]).astype(bf16)
    early = exchange_start(d_out_buf, inner_chunk(dxc), 0)
    early_keys = exchange_start(e_out, chunk(e_in), 1)

    seg_over, seg_down = pair(seg)
    row_allowed = (seg_over == seg_down) & (down // TILE == over // TILE)

    loads[5].wait()
    loads[6].wait()
    row_inv, rq, rk, rv = project(xr, row_gain, rw, arrival(xr, 0, cells_out))
    exchange_wait(early)
    exchange_wait(early_keys)
    d_spread = spread_start(dxc, 1)
    row_att = attend(rq, rk, rv, row_allowed, p_row)
    loads[7].wait()

    def row_term(c):
        return dot(row_att, ro[:, lanes(c)])

    bufs = (r_sib, r_got, r_x, r_xgot)
    state = sum_start(row_term, bufs, 0)
    d_spread = spread_relay(dxc, 1, d_spread)
    mixed = (xr[me].astype(f32) + sum_end(row_term, bufs, state)).astype(bf16)
    m_out[...] = dot(place, mixed).astype(bf16)
    arriving = exchange_start(m_out, inner_chunk(xc), 2)

    marks_in = e_in[...]
    col_allowed = dot_nt(marks_in, marks_in) > 0.5
    col_allowed = col_allowed | (
        lax.broadcasted_iota(jnp.int32, (slots, slots), 0)
        == lax.broadcasted_iota(jnp.int32, (slots, slots), 1)
    )
    for i in (8, 9, 10):
        loads[i].wait()
    moved = []
    for d in range(bands):
        if d:
            arriving[d - 1].wait_recv()
        at = pl.ds(pl.multiple_of(lax.rem(band + bands - d, bands) * cap, 16), cap)
        mine = xc.at[me, at]
        across = send(mine, mine, fw_send.at[d, 0], fw_recv.at[d, 0], (band, far))
        beside = send(mine, mine, fw_send.at[d, 1], fw_recv.at[d, 1], (band, near))
        moved.append((at, across, beside))
    spread_wait(d_spread)
    relays = []

    def all_near():
        for _, _, beside in moved:
            beside.wait_recv()

    def all_far():
        for d, (at, across, _) in enumerate(moved):
            across.wait_recv()
            theirs = xc.at[far, at]
            relays.append(
                send(theirs, theirs, fw_send.at[d, 2], fw_recv.at[d, 2], (band, near))
            )

    def all_corner():
        spread_wait(relays)

    col_inv, cq, ck, cv = project(
        xc, col_gain, cw, ((me, nothing), (near, all_near), (far, all_far), (corner, all_corner))
    )
    col_att = attend(cq, ck, cv, col_allowed, p_col)

    def col_term(c):
        return dot(col_att, co[:, lanes(c)])

    fwd_bufs = (c_sib, c_got, c_x, c_xgot)
    first = sum_open(col_term, fwd_bufs, 1)
    fwd = []

    def between():
        fwd.extend(sum_cross(col_term, fwd_bufs, 1, first))

    landed = tuple((c, nothing) for c in range(groups))
    col_part = back(
        xc, dxc, col_inv, col_gain, cw, co, cq, ck, cv, p_col, dn_col, landed, between
    )
    bwd_bufs = (b_sib, b_got, b_x, b_xgot)
    bwd = sum_start(col_part, bwd_bufs, 2)
    g_out[...] = (dxc[me].astype(f32) + sum_end(col_part, bwd_bufs, bwd)).astype(bf16)
    g_copies = exchange_start(g_out, chunk(g_back), 3)
    s_out[...] = (xc[me].astype(f32) + sum_end(col_term, fwd_bufs, fwd)).astype(bf16)
    s_copies = exchange_start(s_out, chunk(s_back), 4)
    exchange_wait(g_copies)
    dxr[me] = dot_tn(place, g_back[...]).astype(bf16)
    last = spread_start(dxr, 3)

    def write_result():
        exchange_wait(s_copies)
        result[...] = dot_tn(place, s_back[...]).astype(bf16)


    row_part = back(
        xr, dxr, row_inv, row_gain, rw, ro, rq, rk, rv, p_row, dn_row,
        arrival(dxr, 3, last), write_result,
    )
    end_bufs = (q_sib, q_got, q_x, q_xgot)
    end = sum_start(row_part, end_bufs, 3)
    d_cells[...] = (dxr[me].astype(f32) + sum_end(row_part, end_bufs, end)).astype(bf16)
    for copy in pending:
        copy.wait_send()


def fused(bands, cells, row_gain, row_qkv, row_out, col_gain, col_qkv, col_out, row_seg, col_dest, index, d_result):
    rows, width = cells.shape
    features = row_out.shape[1]
    groups = features // width
    heads = width // HEAD_DIM
    cap = 3 * rows // (2 * bands)
    slots = bands * cap
    vmem = pl.BlockSpec(memory_space=pltpu.VMEM)
    hbm = pl.BlockSpec(memory_space=pltpu.HBM)

    def sum_bufs(n):
        return [
            pltpu.VMEM((2, n, width), bf16), pltpu.VMEM((2, n, width), bf16),
            pltpu.VMEM((n, width), bf16), pltpu.VMEM((n, width), bf16),
        ]

    return pl.pallas_call(
        functools.partial(fused_kernel, bands, cap),
        out_shape=(
            jax.ShapeDtypeStruct(cells.shape, bf16),
            jax.ShapeDtypeStruct(cells.shape, bf16),
        ),
        in_specs=[hbm] * 11,
        out_specs=(vmem, vmem),
        scratch_shapes=[
            pltpu.VMEM(d_result.shape, bf16),
            pltpu.VMEM((groups, 1, width), f32), pltpu.VMEM((groups, 1, width), f32),
            *[pltpu.VMEM((1, rows), jnp.int32) for _ in range(3)],
            pltpu.VMEM(row_qkv.shape, bf16), pltpu.VMEM(row_out.shape, bf16),
            pltpu.VMEM(col_qkv.shape, bf16), pltpu.VMEM(col_out.shape, bf16),
            pltpu.VMEM((groups, rows, width), bf16), pltpu.VMEM((groups, slots, width), bf16),
            pltpu.VMEM((groups, slots, width), bf16), pltpu.VMEM((groups, rows, width), bf16),
            pltpu.VMEM((slots, KEY_LANES), bf16), pltpu.VMEM((slots, KEY_LANES), bf16),
            *[pltpu.VMEM((slots, width), bf16) for _ in range(6)],
            *sum_bufs(rows), *sum_bufs(slots), *sum_bufs(slots), *sum_bufs(rows),
            pltpu.VMEM((heads, rows, rows), f32), pltpu.VMEM((heads, slots, slots), f32),
            pltpu.VMEM((groups, rows, width), bf16), pltpu.VMEM((groups, slots, width), bf16),
            pltpu.SemaphoreType.DMA((11,)),
            pltpu.SemaphoreType.DMA((bands, 3)), pltpu.SemaphoreType.DMA((bands, 3)),
            pltpu.SemaphoreType.DMA((4, 3)), pltpu.SemaphoreType.DMA((4, 3)),
            pltpu.SemaphoreType.DMA((4, 3)), pltpu.SemaphoreType.DMA((4, 3)),
            pltpu.SemaphoreType.DMA((5, bands)), pltpu.SemaphoreType.DMA((5, bands)),
        ],
        compiler_params=pltpu.CompilerParams(
            collective_id=0, has_side_effects=True, vmem_limit_bytes=60 * 1024 * 1024
        ),
        cost_estimate=pl.CostEstimate(flops=8 * 10**9, bytes_accessed=5 * 10**6, transcendentals=10**6),
    )(
        cells, d_result,
        row_gain.reshape(groups, 1, width), col_gain.reshape(groups, 1, width),
        row_seg.reshape(1, rows), col_dest.reshape(1, rows), index.reshape(1, rows),
        row_qkv, row_out, col_qkv, col_out,
    )


def block_terms(inputs, norm_gain, query_key_value_weight, w_out, allowed, tile_rows):
    values = inputs.astype(jnp.float32)
    inv_rms = lax.rsqrt(jnp.mean(values * values, axis=-1, keepdims=True) + norm_eps)
    normalized_cells = (values * inv_rms * norm_gain).astype(jnp.bfloat16)
    projected_heads = jnp.einsum(
        "lu,xuh->xlh", normalized_cells, query_key_value_weight, preferred_element_type=jnp.float32
    ).astype(jnp.bfloat16)
    row_count = inputs.shape[0]
    feat_width = query_key_value_weight.shape[2]
    head_count = feat_width // HEAD_DIM
    shaped = projected_heads.reshape(3, row_count // tile_rows, tile_rows, head_count, HEAD_DIM)
    scores = jnp.einsum(
        "bqhe,bkhe->bhqk", shaped[0], shaped[1], preferred_element_type=jnp.float32
    ) * HEAD_DIM ** (-0.5)
    scores = jnp.where(allowed[:, None], scores, neg_fill)
    scores = scores - lax.stop_gradient(jnp.max(scores, axis=-1, keepdims=True))
    expd = jnp.exp(scores)
    attn_probs = (expd / jnp.sum(expd, axis=-1, keepdims=True)).astype(jnp.bfloat16)
    attended = jnp.einsum(
        "bhqk,bkhe->bqhe", attn_probs, shaped[2], preferred_element_type=jnp.float32
    ).astype(jnp.bfloat16)
    attended = attended.reshape(row_count, feat_width)
    return jnp.dot(attended, w_out, preferred_element_type=jnp.float32)


def column_band_mask(col_keys):
    positions = jnp.arange(col_keys.shape[0])
    same_col = (col_keys[:, None] == col_keys[None, :]) & (col_keys[None, :] > 0)
    return (same_col | (positions[:, None] == positions[None, :]))[None]


def widen(block):
    return lax.all_gather(block, "mp", axis=1, tiled=True)


def narrow(terms):
    return lax.psum_scatter(
        terms.astype(jnp.bfloat16), "mp", scatter_dimension=1, tiled=True
    ).astype(jnp.float32)


def move_rows(rows):
    return lax.all_to_all(rows, "band", split_axis=0, concat_axis=0, tiled=True)


def on_device(
    cells,
    row_gain,
    row_qkv,
    row_out,
    col_gain,
    col_qkv,
    col_out,
    row_seg,
    col_dest,
    sheet_column_index,
    d_result,
):
    cell_rows, feat_width = cells.shape
    band_count = lax.axis_size("band")
    capacity = max(2, 3 * cell_rows // (2 * band_count))
    slot_total = band_count * capacity
    spare = (3 * cell_rows) % (2 * band_count) or capacity % 16
    if lax.axis_size("mp") == 4 and cell_rows == 2 * TILE and not spare:
        return fused(
            band_count, cells, row_gain, row_qkv, row_out, col_gain, col_qkv, col_out,
            row_seg, col_dest, sheet_column_index, d_result,
        )
    gathered = widen(cells)
    row_groups = row_seg.reshape(cell_rows // TILE, TILE)
    row_mask = row_groups[:, :, None] == row_groups[:, None, :]

    def row_local(inputs):
        return block_terms(inputs, row_gain, row_qkv, row_out, row_mask, TILE)

    row_terms, row_pull = jax.vjp(row_local, gathered)
    target = col_dest[:, 0]
    place = jnp.arange(cell_rows, dtype=jnp.int32)
    earlier = (target[:, None] == target[None, :]) & (place[None, :] < place[:, None])
    ranking = jnp.sum(earlier.astype(jnp.int32), axis=1)
    slot_index = target * capacity + ranking
    keys_out = (
        jnp.zeros((slot_total,), jnp.bfloat16)
        .at[slot_index]
        .set(sheet_column_index.astype(jnp.bfloat16))
    )
    back_in = jnp.zeros((slot_total, feat_width), jnp.bfloat16).at[slot_index].set(d_result)
    mixed_rows = (cells.astype(jnp.float32) + narrow(row_terms)).astype(jnp.bfloat16)
    outgoing = jnp.zeros((slot_total, feat_width), jnp.bfloat16).at[slot_index].set(mixed_rows)
    arrived, col_keys = (
        lax.all_to_all(outgoing, "band", split_axis=0, concat_axis=0, tiled=True),
        lax.all_to_all(keys_out, "band", split_axis=0, concat_axis=0, tiled=True),
    )
    column_full = widen(arrived)
    col_allowed = column_band_mask(col_keys)

    def col_local(inputs):
        return block_terms(inputs, col_gain, col_qkv, col_out, col_allowed, inputs.shape[0])

    col_terms, col_pull = jax.vjp(col_local, column_full)
    settled = (arrived.astype(jnp.float32) + narrow(col_terms)).astype(jnp.bfloat16)
    result = move_rows(settled)[slot_index]
    d_column = move_rows(back_in)
    (d_col_part,) = col_pull(widen(d_column).astype(jnp.float32))
    d_mixed_col = (d_column.astype(jnp.float32) + narrow(d_col_part.astype(jnp.float32))).astype(
        jnp.bfloat16
    )
    d_mixed = move_rows(d_mixed_col)[slot_index]
    (d_row_part,) = row_pull(widen(d_mixed).astype(jnp.float32))
    d_cells = (d_mixed.astype(jnp.float32) + narrow(d_row_part.astype(jnp.float32))).astype(
        jnp.bfloat16
    )
    return (result, d_cells)


def solution(mesh):
    in_specs = (
        P("band", "mp"),
        P(),
        P(None, None, "mp"),
        P("mp", None),
        P(),
        P(None, None, "mp"),
        P("mp", None),
        P("band"),
        P("band", None),
        P("band"),
        P("band", "mp"),
    )
    out_specs = (P("band", "mp"), P("band", "mp"))
    return jax.shard_map(
        on_device, mesh=mesh, in_specs=in_specs, out_specs=out_specs, check_vma=False
    )
```

```python
import functools

import jax
import jax.numpy as jnp
from jax import lax
from jax.experimental import pallas as pl
from jax.experimental.pallas import tpu as pltpu
from jax.sharding import PartitionSpec as P

HEAD_DIM = 64
TILE = 128


norm_eps = 1e-06
neg_fill = -1e30

MESH = pl.DeviceIdType.MESH
KEY_LANES = 128
f32, bf16 = jnp.float32, jnp.bfloat16


def dot(a, b):
    return lax.dot_general(a, b, (((1,), (0,)), ((), ())), preferred_element_type=f32)


def dot_nt(a, b):
    return lax.dot_general(a, b, (((1,), (1,)), ((), ())), preferred_element_type=f32)


def dot_tn(a, b):
    return lax.dot_general(a, b, (((0,), (0,)), ((), ())), preferred_element_type=f32)


def fused_kernel(
    bands, cap,
    cells, d_any, rg_any, cg_any, seg_any, dest_any, key_any, rw_any, ro_any, cw_any, co_any,
    both,
    d_result, row_gain, col_gain, seg, dest, key, rw, ro, cw, co, xr, xc, dxc, dxr, e_out, e_in,
    d_out_buf, m_out, s_out, g_out, s_back, g_back,
    r_sib, r_got, r_x, r_xgot, c_sib, c_got, c_x, c_xgot,
    b_sib, b_got, b_x, b_xgot, q_sib, q_got, q_x, q_xgot,
    p_row, p_col, dn_row, dn_col,
    w_sem, fw_send, fw_recv, ag_send, ag_recv, rs_send, rs_recv, aa_send, aa_recv,
):
    rows, width = cells.shape
    groups = xr.shape[0]
    slots = bands * cap
    heads = width // HEAD_DIM
    features = groups * width
    band, me = lax.axis_index("band"), lax.axis_index("mp")
    near = me + 1 - 2 * lax.rem(me, 2)
    far = lax.rem(me + 2, 4)
    corner = lax.rem(near + 2, 4)
    pending = []

    loads = []
    for i, (src, dst) in enumerate((
        (cells, xr.at[me]), (dest_any, dest), (key_any, key), (d_any, d_result), (seg_any, seg),
        (rg_any, row_gain), (rw_any, rw), (ro_any, ro), (cg_any, col_gain), (cw_any, cw), (co_any, co),
    )):
        load = pltpu.make_async_copy(src, dst, w_sem.at[i])
        load.start()
        loads.append(load)

    barrier = pltpu.get_barrier_semaphore()
    for peer in (near, far):
        pl.semaphore_signal(barrier, inc=1, device_id=(band, peer), device_id_type=MESH)
    for d in range(1, bands):
        pl.semaphore_signal(
            barrier, inc=1, device_id=(lax.rem(band + d, bands), me), device_id_type=MESH
        )
    pl.semaphore_wait(barrier, bands + 1)

    def send(src, dst, send_sem, recv_sem, to):
        copy = pltpu.make_async_remote_copy(
            src_ref=src, dst_ref=dst, send_sem=send_sem, recv_sem=recv_sem,
            device_id=to, device_id_type=MESH,
        )
        copy.start()
        pending.append(copy)
        return copy

    def spread_start(buf, n):
        across = send(buf.at[me], buf.at[me], ag_send.at[n, 0], ag_recv.at[n, 0], (band, far))
        beside = send(buf.at[me], buf.at[me], ag_send.at[n, 1], ag_recv.at[n, 1], (band, near))
        return across, beside

    def spread_relay(buf, n, started):
        across, beside = started
        across.wait_recv()
        relay = send(buf.at[far], buf.at[far], ag_send.at[n, 2], ag_recv.at[n, 2], (band, near))
        return beside, relay

    def nothing():
        return None

    def arrival(buf, n, started):
        across, beside = started
        held = []

        def cross():
            held.append(spread_relay(buf, n, started)[1])

        def turn():
            held[0].wait_recv()

        return ((me, nothing), (near, beside.wait_recv), (far, cross), (corner, turn))

    def spread_wait(copies):
        for copy in copies:
            copy.wait_recv()

    def exchange_start(src, dst_at, n):
        copies = []
        for d in range(1, bands):
            to = lax.rem(band + d, bands)
            copies.append(
                send(src.at[pl.ds(pl.multiple_of(to * cap, 16), cap)], dst_at(band),
                     aa_send.at[n, d], aa_recv.at[n, d], (to, me))
            )
        dst_at(band)[...] = src[pl.ds(pl.multiple_of(band * cap, 16), cap), :]
        return copies

    def exchange_wait(copies):
        for copy in copies:
            copy.wait_recv()

    def chunk(ref):
        return lambda s: ref.at[pl.ds(pl.multiple_of(s * cap, 16), cap)]

    def inner_chunk(ref):
        return lambda s: ref.at[me, pl.ds(pl.multiple_of(s * cap, 16), cap)]

    def sum_start(part, bufs, n):
        return sum_cross(part, bufs, n, sum_open(part, bufs, n))

    def sum_open(part, bufs, n):
        sib, got, _, _ = bufs
        sib[0] = part(corner).astype(bf16)
        return send(sib.at[0], got.at[0], rs_send.at[n, 0], rs_recv.at[n, 0], (band, near))

    def sum_cross(part, bufs, n, a):
        sib, got, out, arrived = bufs
        mine = part(far)
        a.wait_recv()
        out[...] = (mine + got[0].astype(f32)).astype(bf16)
        c = send(out, arrived, rs_send.at[n, 2], rs_recv.at[n, 2], (band, far))
        sib[1] = part(near).astype(bf16)
        b = send(sib.at[1], got.at[1], rs_send.at[n, 1], rs_recv.at[n, 1], (band, near))
        return b, c

    def sum_end(part, bufs, state):
        _, got, _, arrived = bufs
        b, c = state
        own = part(me).astype(bf16).astype(f32)
        b.wait_recv()
        own = own + got[1].astype(f32)
        c.wait_recv()
        return own + arrived[...].astype(f32)

    def lanes(c):
        return pl.ds(pl.multiple_of(c * width, 128), width)

    def features_of(c):
        return pl.ds(pl.multiple_of(c * width, 128), width)

    def project(x, gain, w, order):
        total = jnp.zeros((x.shape[1], 1), f32)
        acc = [None] * 3
        for c, ready in order:
            ready()
            v = x[c].astype(f32)
            n = (v * gain[c]).astype(bf16)
            for i in range(3):
                t = dot(n, w[i, features_of(c), :])
                acc[i] = t if acc[i] is None else acc[i] + t
            total = total + jnp.sum(v * v, axis=-1, keepdims=True)
        inv = lax.rsqrt(total / features + norm_eps)
        q, k, v = ((t * inv).astype(bf16) for t in acc)
        return inv, q, k, v

    head_of = lax.broadcasted_iota(jnp.int32, (1, width), 1) // HEAD_DIM

    def only(h, t):
        return jnp.where(head_of == h, t, jnp.zeros_like(t))

    def attend(q, k, v, allowed, saved):
        out = None
        for h in range(heads):
            s = dot_nt(only(h, q), k) * HEAD_DIM ** (-0.5)
            s = jnp.where(allowed, s, neg_fill)
            e = jnp.exp(s - jnp.max(s, axis=-1, keepdims=True))
            p = e * (1.0 / jnp.sum(e, axis=-1, keepdims=True))
            saved[h] = p
            t = dot(p.astype(bf16), only(h, v))
            out = t if h == 0 else out + t
        return out.astype(bf16)

    def back(x, dx, inv, gain, w, wo, q, k, v, saved, dn, order, between):
        da = None
        for c, ready in order:
            ready()
            t = dot_nt(dx[c], wo[:, lanes(c)])
            da = t if da is None else da + t
        da = da.astype(bf16)
        dq = dk = dv = None
        for h in range(heads):
            dah = only(h, da)
            p = saved[h]
            dp = dot_nt(dah, v)
            tv = dot_tn(p.astype(bf16), dah)
            ds = p * (dp - jnp.sum(dp * p, axis=-1, keepdims=True))
            ds = (ds * HEAD_DIM ** (-0.5)).astype(bf16)
            tq = dot(ds, only(h, k))
            tk = dot_tn(ds, only(h, q))
            dq, dk, dv = (tq, tk, tv) if h == 0 else (dq + tq, dk + tk, dv + tv)
            if h == 1:
                between()
        dq, dk, dv = dq.astype(bf16), dk.astype(bf16), dv.astype(bf16)
        total = jnp.zeros((x.shape[1], 1), f32)
        for c in range(groups):
            at = slice(c * width, (c + 1) * width)
            g = dot_nt(dq, w[0, at, :]) + dot_nt(dk, w[1, at, :]) + dot_nt(dv, w[2, at, :])
            g = g.astype(bf16)
            dn[c] = g
            total = total + jnp.sum(x[c].astype(f32) * (g.astype(f32) * gain[c]), axis=-1, keepdims=True)
        slope = inv * inv * inv * total * (1.0 / features)

        def part(c):
            return inv * (dn[c].astype(f32) * gain[c]) - x[c].astype(f32) * slope

        return part

    loads[0].wait()
    cells_out = spread_start(xr, 0)

    down = lax.broadcasted_iota(jnp.int32, (rows, rows), 0)
    over = lax.broadcasted_iota(jnp.int32, (rows, rows), 1)

    def pair(ref):
        along = jnp.broadcast_to(ref[...].astype(f32), (rows, rows))
        return along, along.T

    for i in (1, 2, 3, 4):
        loads[i].wait()
    to_over, to_down = pair(dest)
    same = to_over == to_down
    rank_over = jnp.sum(jnp.where(same & (down < over), 1.0, 0.0), axis=0, keepdims=True)
    slot_over = to_over[0:1, :] * cap + rank_over
    at_slot = lax.broadcasted_iota(jnp.int32, (slots, rows), 0).astype(f32)
    place = jnp.where(at_slot == slot_over, 1.0, 0.0).astype(bf16)
    _, key_down = pair(key)
    lane = lax.broadcasted_iota(jnp.int32, (rows, KEY_LANES), 1).astype(f32)
    marks = jnp.where(key_down[:, :KEY_LANES] == lane, 1.0, 0.0).astype(bf16)
    e_out[...] = dot(place, marks).astype(bf16)
    d_out_buf[...] = dot(place, d_result[...]).astype(bf16)
    early = exchange_start(d_out_buf, inner_chunk(dxc), 0)
    early_keys = exchange_start(e_out, chunk(e_in), 1)

    seg_over, seg_down = pair(seg)
    row_allowed = (seg_over == seg_down) & (down // TILE == over // TILE)

    loads[5].wait()
    loads[6].wait()
    row_inv, rq, rk, rv = project(xr, row_gain, rw, arrival(xr, 0, cells_out))
    exchange_wait(early)
    exchange_wait(early_keys)
    d_spread = spread_start(dxc, 1)
    row_att = attend(rq, rk, rv, row_allowed, p_row)
    loads[7].wait()

    def row_term(c):
        return dot(row_att, ro[:, lanes(c)])

    bufs = (r_sib, r_got, r_x, r_xgot)
    state = sum_start(row_term, bufs, 0)
    d_spread = spread_relay(dxc, 1, d_spread)
    mixed = (xr[me].astype(f32) + sum_end(row_term, bufs, state)).astype(bf16)
    m_out[...] = dot(place, mixed).astype(bf16)
    arriving = exchange_start(m_out, inner_chunk(xc), 2)

    marks_in = e_in[...]
    col_allowed = dot_nt(marks_in, marks_in) > 0.5
    col_allowed = col_allowed | (
        lax.broadcasted_iota(jnp.int32, (slots, slots), 0)
        == lax.broadcasted_iota(jnp.int32, (slots, slots), 1)
    )
    for i in (8, 9, 10):
        loads[i].wait()
    moved = []
    for d in range(bands):
        if d:
            arriving[d - 1].wait_recv()
        at = pl.ds(pl.multiple_of(lax.rem(band + bands - d, bands) * cap, 16), cap)
        mine = xc.at[me, at]
        across = send(mine, mine, fw_send.at[d, 0], fw_recv.at[d, 0], (band, far))
        beside = send(mine, mine, fw_send.at[d, 1], fw_recv.at[d, 1], (band, near))
        moved.append((at, across, beside))
    spread_wait(d_spread)
    relays = []

    def all_near():
        for _, _, beside in moved:
            beside.wait_recv()

    def all_far():
        for d, (at, across, _) in enumerate(moved):
            across.wait_recv()
            theirs = xc.at[far, at]
            relays.append(
                send(theirs, theirs, fw_send.at[d, 2], fw_recv.at[d, 2], (band, near))
            )

    def all_corner():
        spread_wait(relays)

    col_inv, cq, ck, cv = project(
        xc, col_gain, cw, ((me, nothing), (near, all_near), (far, all_far), (corner, all_corner))
    )
    col_att = attend(cq, ck, cv, col_allowed, p_col)

    def col_term(c):
        return dot(col_att, co[:, lanes(c)])

    fwd_bufs = (c_sib, c_got, c_x, c_xgot)
    first = sum_open(col_term, fwd_bufs, 1)
    fwd = []

    def between():
        fwd.extend(sum_cross(col_term, fwd_bufs, 1, first))

    landed = tuple((c, nothing) for c in range(groups))
    col_part = back(
        xc, dxc, col_inv, col_gain, cw, co, cq, ck, cv, p_col, dn_col, landed, between
    )
    bwd_bufs = (b_sib, b_got, b_x, b_xgot)
    bwd = sum_start(col_part, bwd_bufs, 2)
    g_out[...] = (dxc[me].astype(f32) + sum_end(col_part, bwd_bufs, bwd)).astype(bf16)
    g_copies = exchange_start(g_out, chunk(g_back), 3)
    s_out[...] = (xc[me].astype(f32) + sum_end(col_term, fwd_bufs, fwd)).astype(bf16)
    s_copies = exchange_start(s_out, chunk(s_back), 4)
    exchange_wait(g_copies)
    dxr[me] = dot_tn(place, g_back[...]).astype(bf16)
    last = spread_start(dxr, 3)

    def write_result():
        exchange_wait(s_copies)
        both[0] = dot_tn(place, s_back[...]).astype(bf16)


    row_part = back(
        xr, dxr, row_inv, row_gain, rw, ro, rq, rk, rv, p_row, dn_row,
        arrival(dxr, 3, last), write_result,
    )
    end_bufs = (q_sib, q_got, q_x, q_xgot)
    end = sum_start(row_part, end_bufs, 3)
    both[1] = (dxr[me].astype(f32) + sum_end(row_part, end_bufs, end)).astype(bf16)
    for copy in pending:
        copy.wait_send()


def fused(bands, cells, row_gain, row_qkv, row_out, col_gain, col_qkv, col_out, row_seg, col_dest, index, d_result):
    rows, width = cells.shape
    features = row_out.shape[1]
    groups = features // width
    heads = width // HEAD_DIM
    cap = 3 * rows // (2 * bands)
    slots = bands * cap
    vmem = pl.BlockSpec(memory_space=pltpu.VMEM)
    hbm = pl.BlockSpec(memory_space=pltpu.HBM)

    def sum_bufs(n):
        return [
            pltpu.VMEM((2, n, width), bf16), pltpu.VMEM((2, n, width), bf16),
            pltpu.VMEM((n, width), bf16), pltpu.VMEM((n, width), bf16),
        ]

    both = pl.pallas_call(
        functools.partial(fused_kernel, bands, cap),
        out_shape=jax.ShapeDtypeStruct((2, *cells.shape), bf16),
        in_specs=[hbm] * 11,
        out_specs=vmem,
        scratch_shapes=[
            pltpu.VMEM(d_result.shape, bf16),
            pltpu.VMEM((groups, 1, width), f32), pltpu.VMEM((groups, 1, width), f32),
            *[pltpu.VMEM((1, rows), jnp.int32) for _ in range(3)],
            pltpu.VMEM(row_qkv.shape, bf16), pltpu.VMEM(row_out.shape, bf16),
            pltpu.VMEM(col_qkv.shape, bf16), pltpu.VMEM(col_out.shape, bf16),
            pltpu.VMEM((groups, rows, width), bf16), pltpu.VMEM((groups, slots, width), bf16),
            pltpu.VMEM((groups, slots, width), bf16), pltpu.VMEM((groups, rows, width), bf16),
            pltpu.VMEM((slots, KEY_LANES), bf16), pltpu.VMEM((slots, KEY_LANES), bf16),
            *[pltpu.VMEM((slots, width), bf16) for _ in range(6)],
            *sum_bufs(rows), *sum_bufs(slots), *sum_bufs(slots), *sum_bufs(rows),
            pltpu.VMEM((heads, rows, rows), f32), pltpu.VMEM((heads, slots, slots), f32),
            pltpu.VMEM((groups, rows, width), bf16), pltpu.VMEM((groups, slots, width), bf16),
            pltpu.SemaphoreType.DMA((11,)),
            pltpu.SemaphoreType.DMA((bands, 3)), pltpu.SemaphoreType.DMA((bands, 3)),
            pltpu.SemaphoreType.DMA((4, 3)), pltpu.SemaphoreType.DMA((4, 3)),
            pltpu.SemaphoreType.DMA((4, 3)), pltpu.SemaphoreType.DMA((4, 3)),
            pltpu.SemaphoreType.DMA((5, bands)), pltpu.SemaphoreType.DMA((5, bands)),
        ],
        compiler_params=pltpu.CompilerParams(
            collective_id=0, has_side_effects=True, vmem_limit_bytes=60 * 1024 * 1024
        ),
        cost_estimate=pl.CostEstimate(flops=8 * 10**9, bytes_accessed=5 * 10**6, transcendentals=10**6),
    )(
        cells, d_result,
        row_gain.reshape(groups, 1, width), col_gain.reshape(groups, 1, width),
        row_seg.reshape(1, rows), col_dest.reshape(1, rows), index.reshape(1, rows),
        row_qkv, row_out, col_qkv, col_out,
    )
    return both[0], both[1]


def block_terms(inputs, norm_gain, query_key_value_weight, w_out, allowed, tile_rows):
    values = inputs.astype(jnp.float32)
    inv_rms = lax.rsqrt(jnp.mean(values * values, axis=-1, keepdims=True) + norm_eps)
    normalized_cells = (values * inv_rms * norm_gain).astype(jnp.bfloat16)
    projected_heads = jnp.einsum(
        "lu,xuh->xlh", normalized_cells, query_key_value_weight, preferred_element_type=jnp.float32
    ).astype(jnp.bfloat16)
    row_count = inputs.shape[0]
    feat_width = query_key_value_weight.shape[2]
    head_count = feat_width // HEAD_DIM
    shaped = projected_heads.reshape(3, row_count // tile_rows, tile_rows, head_count, HEAD_DIM)
    scores = jnp.einsum(
        "bqhe,bkhe->bhqk", shaped[0], shaped[1], preferred_element_type=jnp.float32
    ) * HEAD_DIM ** (-0.5)
    scores = jnp.where(allowed[:, None], scores, neg_fill)
    scores = scores - lax.stop_gradient(jnp.max(scores, axis=-1, keepdims=True))
    expd = jnp.exp(scores)
    attn_probs = (expd / jnp.sum(expd, axis=-1, keepdims=True)).astype(jnp.bfloat16)
    attended = jnp.einsum(
        "bhqk,bkhe->bqhe", attn_probs, shaped[2], preferred_element_type=jnp.float32
    ).astype(jnp.bfloat16)
    attended = attended.reshape(row_count, feat_width)
    return jnp.dot(attended, w_out, preferred_element_type=jnp.float32)


def column_band_mask(col_keys):
    positions = jnp.arange(col_keys.shape[0])
    same_col = (col_keys[:, None] == col_keys[None, :]) & (col_keys[None, :] > 0)
    return (same_col | (positions[:, None] == positions[None, :]))[None]


def widen(block):
    return lax.all_gather(block, "mp", axis=1, tiled=True)


def narrow(terms):
    return lax.psum_scatter(
        terms.astype(jnp.bfloat16), "mp", scatter_dimension=1, tiled=True
    ).astype(jnp.float32)


def move_rows(rows):
    return lax.all_to_all(rows, "band", split_axis=0, concat_axis=0, tiled=True)


def on_device(
    cells,
    row_gain,
    row_qkv,
    row_out,
    col_gain,
    col_qkv,
    col_out,
    row_seg,
    col_dest,
    sheet_column_index,
    d_result,
):
    cell_rows, feat_width = cells.shape
    band_count = lax.axis_size("band")
    capacity = max(2, 3 * cell_rows // (2 * band_count))
    slot_total = band_count * capacity
    spare = (3 * cell_rows) % (2 * band_count) or capacity % 16
    if lax.axis_size("mp") == 4 and cell_rows == 2 * TILE and not spare:
        return fused(
            band_count, cells, row_gain, row_qkv, row_out, col_gain, col_qkv, col_out,
            row_seg, col_dest, sheet_column_index, d_result,
        )
    gathered = widen(cells)
    row_groups = row_seg.reshape(cell_rows // TILE, TILE)
    row_mask = row_groups[:, :, None] == row_groups[:, None, :]

    def row_local(inputs):
        return block_terms(inputs, row_gain, row_qkv, row_out, row_mask, TILE)

    row_terms, row_pull = jax.vjp(row_local, gathered)
    target = col_dest[:, 0]
    place = jnp.arange(cell_rows, dtype=jnp.int32)
    earlier = (target[:, None] == target[None, :]) & (place[None, :] < place[:, None])
    ranking = jnp.sum(earlier.astype(jnp.int32), axis=1)
    slot_index = target * capacity + ranking
    keys_out = (
        jnp.zeros((slot_total,), jnp.bfloat16)
        .at[slot_index]
        .set(sheet_column_index.astype(jnp.bfloat16))
    )
    back_in = jnp.zeros((slot_total, feat_width), jnp.bfloat16).at[slot_index].set(d_result)
    mixed_rows = (cells.astype(jnp.float32) + narrow(row_terms)).astype(jnp.bfloat16)
    outgoing = jnp.zeros((slot_total, feat_width), jnp.bfloat16).at[slot_index].set(mixed_rows)
    arrived, col_keys = (
        lax.all_to_all(outgoing, "band", split_axis=0, concat_axis=0, tiled=True),
        lax.all_to_all(keys_out, "band", split_axis=0, concat_axis=0, tiled=True),
    )
    column_full = widen(arrived)
    col_allowed = column_band_mask(col_keys)

    def col_local(inputs):
        return block_terms(inputs, col_gain, col_qkv, col_out, col_allowed, inputs.shape[0])

    col_terms, col_pull = jax.vjp(col_local, column_full)
    settled = (arrived.astype(jnp.float32) + narrow(col_terms)).astype(jnp.bfloat16)
    result = move_rows(settled)[slot_index]
    d_column = move_rows(back_in)
    (d_col_part,) = col_pull(widen(d_column).astype(jnp.float32))
    d_mixed_col = (d_column.astype(jnp.float32) + narrow(d_col_part.astype(jnp.float32))).astype(
        jnp.bfloat16
    )
    d_mixed = move_rows(d_mixed_col)[slot_index]
    (d_row_part,) = row_pull(widen(d_mixed).astype(jnp.float32))
    d_cells = (d_mixed.astype(jnp.float32) + narrow(d_row_part.astype(jnp.float32))).astype(
        jnp.bfloat16
    )
    return (result, d_cells)


def solution(mesh):
    in_specs = (
        P("band", "mp"),
        P(),
        P(None, None, "mp"),
        P("mp", None),
        P(),
        P(None, None, "mp"),
        P("mp", None),
        P("band"),
        P("band", None),
        P("band"),
        P("band", "mp"),
    )
    out_specs = (P("band", "mp"), P("band", "mp"))
    return jax.shard_map(
        on_device, mesh=mesh, in_specs=in_specs, out_specs=out_specs, check_vma=False
    )
```
